32 devices in a mesh: space: 8 (over y, x, core), mode: 4 (over z).
Axes of the slice: x: 2, y: 2, z: 4, core: 2. Of those that a mesh axis runs over, the one named last changes fastest.
Arguments:
- start_field: float32 [36, 16, 64, 128], P('mode', 'space'), may hold values from -1.8 to 1.8
- source: float32 [36, 16, 64, 128], P('mode', 'space')
- mean_field: float32 [16, 64, 128], P('space'), may hold values from 0.5 to 2
- kl_fields: float32 [4, 16, 64, 128], P(None, 'space'), may hold values from -1 to 1
- triples: int32 [156, 3], replicated, may hold values from 0 to 35, as said below
- coef: float32 [156], replicated, may hold values from 0.5 to 2
Outputs:
- smoothed: float32 [36, 16, 64, 128], P('mode', 'space')
- residual: float32 [36, 16, 64, 128], P('mode', 'space')
The draws below stay inside these ranges and needn't reach their ends.
Inputs may be any that keep to these rules, and one draw needn't show every extreme that they name: Rows of triples are distinct. Field 0 appears only in the rows (0, s, s), one for every slot s of the 36 slots; the other rows name a field 1 to 4 and two different slots.
All inputs are finite; a program needn't handle non-finite values.
Results may differ from the reference program's by a relative error of at most 0.00022.
Values sent between devices are 32-bit elements; how exact they have to be, the bound alone decides.
A program may use at most 64 MiB of HBM per device.

```python
import math
import jax
import jax.numpy as jnp
import numpy as np
from jax import lax

VARS = 4
DEGREE = 3
KL = 5
PS = 36
NNZ = 156
NX = 64
NY = 128
NZ = 16


def hermite_pairs():
    multis = []
    for first in range(DEGREE + 1):
        for second in range(DEGREE + 1 - first):
            for third in range(DEGREE + 1 - first - second):
                for fourth in range(DEGREE + 1 - first - second - third):
                    multis.append((first, second, third, fourth))
    multis.sort(key=lambda item: (item[0] + item[1] + item[2] + item[3], item))
    lookup = {}
    for number, item in enumerate(multis):
        lookup[item] = number
    rows_out = []
    for item in multis:
        if item[0] + item[1] + item[2] + item[3] < DEGREE:
            for which in range(VARS):
                raised = list(item)
                raised[which] = raised[which] + 1
                other = lookup[tuple(raised)]
                rows_out.append((which, lookup[item], other))
                rows_out.append((which, other, lookup[item]))
    return np.array(rows_out, dtype=np.int32)


def draw_triples(key, part):
    table = jnp.asarray(hermite_pairs())
    slots = jax.random.permutation(key, PS).astype(jnp.int32)
    variables = jax.random.permutation(jax.random.fold_in(key, 7), VARS).astype(jnp.int32) + 1
    coupled = jnp.stack([variables[table[:, 0]], slots[table[:, 1]], slots[table[:, 2]]], axis=1)
    own_slots = jnp.arange(PS, dtype=jnp.int32)
    mean_rows = jnp.stack([jnp.zeros((PS,), jnp.int32), own_slots, own_slots], axis=1)
    return jnp.concatenate([mean_rows, coupled], axis=0).astype(jnp.int32)


def draw_source(key, part):
    shape = (PS, NZ, NX, NY)
    return jnp.clip(jax.random.normal(key, shape, jnp.float32), -6.0, 6.0)


def block_scale(stream_key, dims, cuts, low, high):
    level, own = 1.0, jax.random.fold_in(stream_key, 6)
    for axis_at, shards_of in cuts:
        draws = jnp.exp(jax.random.uniform(jax.random.fold_in(own, axis_at), (shards_of,), jnp.float32, low / len(cuts), high / len(cuts)))
        level = level * jnp.repeat(draws, dims[axis_at] // shards_of).reshape([-1 if axis == axis_at else 1 for axis in range(len(dims))])
    return level


def noise(own_key, dims, scale, reach, shards=(), kind=jnp.bfloat16):
    gain = block_scale(own_key, dims, shards, -0.22, 0.18) if shards else 1.0
    values = jax.random.normal(own_key, dims, jnp.float32) * scale * gain
    return jnp.minimum(jnp.maximum(values, -reach), reach).astype(kind)


def setup_inputs(seed: int = 0) -> dict:
    splits = jax.random.split(jax.random.key(seed), 7)
    start_field = noise(splits[0], (PS, NZ, NX, NY), 0.3, 1.8, ((0, 4), (1, 8)), jnp.float32)
    source = draw_source(jax.random.fold_in(splits[6], 71), 0)
    mean_field = jnp.clip(jnp.exp(math.log(2.0) - 1.3862944 * jax.random.uniform(splits[2], (NZ, NX, NY), jnp.float32) ** block_scale(splits[2], (NZ, NX, NY), ((0, 8),), -0.2, 0.2)), 0.5, 2.0)
    kl_fields = noise(splits[3], (VARS, NZ, NX, NY), 0.25, 1.0, ((1, 8),), jnp.float32)
    triples = draw_triples(jax.random.fold_in(splits[6], 71), 0)
    coef = jnp.clip(jnp.exp(jax.random.uniform(splits[5], (NNZ,), jnp.float32, math.log(0.5), math.log(2.0))), 0.5, 2.0)
    return dict(start_field=start_field, source=source, mean_field=mean_field, kl_fields=kl_fields, triples=triples, coef=coef)


def neighbour_views(arr):
    return [arr[..., 2:, 1:-1, 1:-1], arr[..., :-2, 1:-1, 1:-1],
            arr[..., 1:-1, 2:, 1:-1], arr[..., 1:-1, :-2, 1:-1],
            arr[..., 1:-1, 1:-1, 2:], arr[..., 1:-1, 1:-1, :-2]]


def stencil(field_pad, coeff_pad):
    centre = field_pad[..., 1:-1, 1:-1, 1:-1]
    own = coeff_pad[..., 1:-1, 1:-1, 1:-1]
    result = None
    for value, other in zip(neighbour_views(field_pad), neighbour_views(coeff_pad)):
        term = 0.5 * (own + other) * (centre - value)
        result = term if result is None else result + term
    return result


def face_total(coeff_pad):
    own = coeff_pad[..., 1:-1, 1:-1, 1:-1]
    result = None
    for other in neighbour_views(coeff_pad):
        term = 0.5 * (own + other)
        result = term if result is None else result + term
    return result


def reference(start_field, source, mean_field, kl_fields, triples, coef):
    coupling = jnp.zeros((KL, PS, PS), jnp.float32).at[triples[:, 0], triples[:, 1], triples[:, 2]].add(coef)
    fields = jnp.concatenate([mean_field[None], kl_fields], axis=0)
    coeff_pad = jnp.pad(fields, ((0, 0), (1, 1), (1, 1), (1, 1)))
    scaling = jnp.diagonal(coupling[0])[:, None, None, None] * face_total(coeff_pad[0])[None]
    per_row = jnp.transpose(coupling, (1, 0, 2))

    def operator(field):
        def one_mode(row):
            mixed = jnp.einsum('mj,jzxy->mzxy', row, field, precision=lax.Precision.HIGHEST)
            mixed_pad = jnp.pad(mixed, ((0, 0), (1, 1), (1, 1), (1, 1)))
            return jnp.sum(stencil(mixed_pad, coeff_pad), axis=0)
        return lax.map(one_mode, per_row)

    first = source - operator(start_field)
    middle = start_field + 0.8 * first / scaling
    residual = source - operator(middle)
    smoothed = middle + 0.8 * residual / scaling
    return smoothed, residual
```

```python
import functools

import jax
import jax.numpy as jnp
from jax import lax
from jax.experimental import pallas as pl
from jax.experimental.pallas import tpu as pltpu
from jax.sharding import PartitionSpec as P

MESH = pl.DeviceIdType.MESH
FACES = 6


def round_up(value, multiple):
    return -(-value // multiple) * multiple


def kernel(
    groups, count, table, start, source, mean, kl,
    a_first, a_second, total_out, diag_out,
    coefs, weights, in_first, in_second, out_first, out_second, vt, cmat,
    trade_send, trade_recv, own_sem, plane_send, plane_recv, row_send, row_recv,
):
    local, planes, height, lanes = start.shape
    slots = local * groups
    rows = height // groups
    nfields = kl.shape[0] + 1
    padded = vt.shape[3]
    entries = weights.shape[0] // (planes * height)
    stride = planes * rows
    me = lax.axis_index("mode")
    at = lax.axis_index("space")
    has_left = at > 0
    has_right = at < count - 1

    barrier = pltpu.get_barrier_semaphore()
    for d in range(1, groups):
        pl.semaphore_signal(
            barrier, inc=1, device_id={"mode": lax.rem(me + d, groups)}, device_id_type=MESH
        )

    @pl.when(has_left)
    def _():
        pl.semaphore_signal(barrier, inc=1, device_id={"space": at - 1}, device_id_type=MESH)

    @pl.when(has_right)
    def _():
        pl.semaphore_signal(barrier, inc=1, device_id={"space": at + 1}, device_id_type=MESH)

    for z in range(planes):
        coefs[z + 1, 0] = mean[z]
        for m in range(1, nfields):
            coefs[z + 1, m] = kl[m - 1, z]

    @pl.when(jnp.logical_not(has_left))
    def _():
        coefs[0] = jnp.zeros(coefs.shape[1:], jnp.float32)
        for k in range(2):
            vt[k, 0] = jnp.zeros(vt.shape[2:], jnp.float32)

    @pl.when(jnp.logical_not(has_right))
    def _():
        coefs[planes + 1] = jnp.zeros(coefs.shape[1:], jnp.float32)
        for k in range(2):
            vt[k, planes + 1] = jnp.zeros(vt.shape[2:], jnp.float32)

    @pl.when(me == 0)
    def _():
        for k in range(2):
            for z in range(planes):
                vt[k, z + 1, 0] = jnp.zeros(vt.shape[3:], jnp.float32)

    @pl.when(me == groups - 1)
    def _():
        for k in range(2):
            for z in range(planes):
                vt[k, z + 1, rows + 1] = jnp.zeros(vt.shape[3:], jnp.float32)

    def band(ref, which):
        return ref.at[:, :, pl.ds(pl.multiple_of(which * rows, rows), rows), :]

    def modes(ref, which):
        size = local * stride
        return ref.at[pl.ds(pl.multiple_of(which * size, size), size), :].reshape(
            local, planes, rows, lanes
        )

    def remote(phase, d):
        peer = lax.rem(me + d, groups)
        if phase < 2:
            src = band((start, source)[phase], peer)
            dst = modes((in_first, in_second)[phase], me)
        else:
            src = modes((out_first, out_second)[phase - 2], peer)
            dst = band((a_first, a_second)[phase - 2], me)
        return pltpu.make_async_remote_copy(
            src_ref=src, dst_ref=dst,
            send_sem=trade_send.at[phase, d - 1], recv_sem=trade_recv.at[phase, d - 1],
            device_id={"mode": peer}, device_id_type=MESH,
        )

    def own(phase):
        if phase < 2:
            src = band((start, source)[phase], me)
            dst = modes((in_first, in_second)[phase], me)
        else:
            src = modes((out_first, out_second)[phase - 2], me)
            dst = band((a_first, a_second)[phase - 2], me)
        return pltpu.make_async_copy(src, dst, own_sem.at[phase])

    def trade_start(phase):
        for d in (2, 1, 3) if groups == 4 else range(1, groups):
            remote(phase, d).start()
        own(phase).start()

    def trade_wait_send(phase):
        for d in range(1, groups):
            remote(phase, d).wait_send()

    def trade_wait_recv(phase):
        for d in range(1, groups):
            remote(phase, d).wait_recv()
        own(phase).wait()

    def plane_copy(k, side):
        if k == 2:
            buf, inner = coefs, lambda z: coefs.at[z]
        else:
            buf, inner = vt, lambda z: vt.at[k, z, pl.ds(1, rows)]
        src, dst = (1, planes + 1) if side == 0 else (planes, 0)
        return pltpu.make_async_remote_copy(
            src_ref=inner(src), dst_ref=inner(dst),
            send_sem=plane_send.at[k, side], recv_sem=plane_recv.at[k, side],
            device_id={"space": at - 1 if side == 0 else at + 1}, device_id_type=MESH,
        )

    def plane_start(k, side):
        @pl.when(has_left if side == 0 else has_right)
        def _():
            plane_copy(k, side).start()

    def plane_wait(k):
        for side, sends, gets in ((0, has_left, has_right), (1, has_right, has_left)):
            @pl.when(sends)
            def _():
                plane_copy(k, side).wait_send()

            @pl.when(gets)
            def _():
                plane_copy(k, side).wait_recv()

    has_up = me > 0
    has_down = me < groups - 1

    def row_copy(k, side):
        src, dst = (1, rows + 1) if side == 0 else (rows, 0)
        return pltpu.make_async_remote_copy(
            src_ref=vt.at[k, pl.ds(1, planes), src], dst_ref=vt.at[k, pl.ds(1, planes), dst],
            send_sem=row_send.at[k, side], recv_sem=row_recv.at[k, side],
            device_id={"mode": me - 1 if side == 0 else me + 1}, device_id_type=MESH,
        )

    def row_start(k):
        for side, sends in ((0, has_up), (1, has_down)):
            @pl.when(sends)
            def _():
                row_copy(k, side).start()

    def row_wait(k):
        for side, sends, gets in ((0, has_up, has_down), (1, has_down, has_up)):
            @pl.when(sends)
            def _():
                row_copy(k, side).wait_send()

            @pl.when(gets)
            def _():
                row_copy(k, side).wait_recv()

    pl.semaphore_wait(
        barrier, groups - 1 + has_left.astype(jnp.int32) + has_right.astype(jnp.int32)
    )
    trade_start(0)
    plane_start(2, 0)
    plane_start(2, 1)

    nnz = table.shape[1]
    width = cmat.shape[1]
    fields_row, rows_row, cols_row, coef_row = (table[i:i + 1, :] for i in range(4))
    row_hot = lax.broadcasted_iota(jnp.int32, (padded, nnz), 0).astype(jnp.float32) == rows_row
    key = fields_row * padded + cols_row
    key_hot = lax.broadcasted_iota(jnp.int32, (width, nnz), 0).astype(jnp.float32) == key
    coef_high = coef_row.astype(jnp.bfloat16).astype(jnp.float32)
    row_one = jnp.where(row_hot, 1.0, 0.0).astype(jnp.bfloat16)
    for piece, value in enumerate((coef_high, coef_row - coef_high)):
        spread = jnp.where(key_hot, value, 0.0).astype(jnp.bfloat16)
        part = lax.dot_general(
            row_one, spread, (((1,), (1,)), ((), ())), preferred_element_type=jnp.float32
        )
        cmat[piece * padded:(piece + 1) * padded, :] = part.astype(jnp.bfloat16)
    diag = jnp.sum(
        jnp.where(jnp.logical_and(row_hot, fields_row == 0.0), coef_row, 0.0), axis=1, keepdims=True
    )
    real = lax.broadcasted_iota(jnp.int32, (padded, 1), 0) < slots
    diag = jnp.where(real, diag, 1.0)
    diag_out[...] = jnp.broadcast_to(diag, diag_out.shape)
    step = 0.8 / diag

    plane_wait(2)
    lane = lax.broadcasted_iota(jnp.int32, (height, lanes), 1)
    row = lax.broadcasted_iota(jnp.int32, (height, lanes), 0)
    for z in range(planes):
        for m in range(nfields):
            c = coefs[z + 1, m]
            faces = []
            for axis, size, ids in ((1, lanes, lane), (0, height, row)):
                for shift, edge in ((size - 1, size - 1), (1, 0)):
                    other = jnp.where(ids == edge, 0.0, pltpu.roll(c, shift, axis))
                    faces.append(0.5 * (c + other))
            faces.append(0.5 * (c + coefs[z + 2, m]))
            faces.append(0.5 * (c + coefs[z, m]))
            total = functools.reduce(lambda a, b: a + b, faces)
            faces[0] = jnp.where(lane == lanes - 1, 0.0, faces[0])
            faces[1] = jnp.where(lane == 0, 0.0, faces[1])
            first = z * height * entries
            for f, value in enumerate(faces + [total]):
                weights[pl.ds(first + f * nfields + m, height, stride=entries), :] = value
            if m == 0:
                total_out[z] = total
                weights[pl.ds(first + (FACES + 1) * nfields, height, stride=entries), :] = 1.0 / total

    trade_wait_send(0)
    trade_start(1)
    trade_wait_recv(0)

    fill = jnp.zeros((padded - slots, lanes), jnp.float32)
    half = rows // 2

    def fetch(ref, z, y):
        return ref[pl.ds(z * rows + y, slots, stride=stride), :]

    def spread_weights(z, y):
        base = pl.multiple_of((z * height + me * rows + y) * entries, 8)
        return weights[pl.ds(base, entries), :]

    for z in range(planes):
        def relay(y, carry):
            vt[0, z + 1, y + 1] = jnp.concatenate([fetch(in_first, z, y), fill], axis=0)
            return carry
        lax.fori_loop(0, rows, relay, 0)
        if z == 0:
            plane_start(0, 0)
        if z == planes - 1:
            plane_start(0, 1)
    row_start(0)

    def applied(k, z, y):
        w = spread_weights(z, y)
        centre = vt[k, z + 1, y + 1]
        others = (
            pltpu.roll(centre, lanes - 1, 1), pltpu.roll(centre, 1, 1),
            vt[k, z + 1, y + 2], vt[k, z + 1, y],
            vt[k, z + 2, y + 1], vt[k, z, y + 1],
        )
        parts = []
        for m in range(nfields):
            at_total = FACES * nfields + m
            value = w[at_total:at_total + 1] * centre
            for f in range(FACES):
                at_face = f * nfields + m
                value = value - w[at_face:at_face + 1] * others[f]
            parts.append(value)
        if width > nfields * padded:
            parts.append(jnp.zeros((width - nfields * padded, lanes), jnp.float32))
        return jnp.concatenate(parts, axis=0)

    def sweep(k, out):
        def pair(t, carry):
            z = t // half
            y = 2 * lax.rem(t, half)
            x = jnp.concatenate([applied(k, z, y), applied(k, z, y + 1)], axis=1)
            high = x.astype(jnp.bfloat16)
            low = (x - high.astype(jnp.float32)).astype(jnp.bfloat16)
            both = jnp.dot(cmat[...], high, preferred_element_type=jnp.float32)
            rest = jnp.dot(cmat[:padded, :], low, preferred_element_type=jnp.float32)
            value = both[:padded] + (both[padded:] + rest)
            for i in range(2):
                out[pl.ds(z * rows + y + i, slots, stride=stride), :] = value[
                    :slots, i * lanes:(i + 1) * lanes
                ]
            return carry
        lax.fori_loop(0, planes * half, pair, 0)

    plane_wait(0)
    row_wait(0)
    sweep(0, out_first)
    trade_wait_recv(1)
    trade_wait_send(1)

    for z in range(planes):
        def update(y, carry):
            inverse = spread_weights(z, y)[(FACES + 1) * nfields:(FACES + 1) * nfields + 1]
            first = fetch(in_second, z, y) - fetch(out_first, z, y)
            first = jnp.concatenate([first, fill], axis=0)
            vt[1, z + 1, y + 1] = vt[0, z + 1, y + 1] + first * (step * inverse)
            return carry
        lax.fori_loop(0, rows, update, 0)
        if z == 0:
            plane_start(1, 0)
        if z == planes - 1:
            plane_start(1, 1)
    row_start(1)
    trade_start(2)
    plane_wait(1)
    row_wait(1)
    sweep(1, out_second)
    trade_start(3)
    for phase in (2, 3):
        trade_wait_send(phase)
        trade_wait_recv(phase)


def body(count, start_field, source, mean_field, kl_fields, triples, coef):
    local, planes, height, lanes = start_field.shape
    groups = lax.axis_size("mode")
    slots = local * groups
    nfields = kl_fields.shape[0] + 1
    rows = height // groups
    padded = round_up(slots, 8)
    width = round_up(nfields * padded, 16)
    entries = round_up((FACES + 1) * nfields + 1, 8)
    table = jnp.concatenate([triples.T.astype(jnp.float32), coef[None]], axis=0)
    f32 = jnp.float32
    whole = jax.ShapeDtypeStruct(start_field.shape, f32)
    in_vmem = pl.BlockSpec(memory_space=pltpu.VMEM)
    anywhere = pl.BlockSpec(memory_space=pl.ANY)
    dma = pltpu.SemaphoreType.DMA
    a_first, a_second, totals, diag = pl.pallas_call(
        functools.partial(kernel, groups, count),
        out_shape=(
            whole, whole,
            jax.ShapeDtypeStruct((planes, height, lanes), f32),
            jax.ShapeDtypeStruct((padded, lanes), f32),
        ),
        in_specs=[in_vmem, anywhere, anywhere, in_vmem, in_vmem],
        out_specs=(anywhere, anywhere, in_vmem, in_vmem),
        scratch_shapes=[
            pltpu.VMEM((planes + 2, nfields, height, lanes), f32),
            pltpu.VMEM((planes * height * entries, lanes), f32),
            pltpu.VMEM((slots * planes * rows, lanes), f32),
            pltpu.VMEM((slots * planes * rows, lanes), f32),
            pltpu.VMEM((slots * planes * rows, lanes), f32),
            pltpu.VMEM((slots * planes * rows, lanes), f32),
            pltpu.VMEM((2, planes + 2, rows + 2, padded, lanes), f32),
            pltpu.VMEM((2 * padded, width), jnp.bfloat16),
            dma((4, groups - 1)), dma((4, groups - 1)), dma((4,)),
            dma((3, 2)), dma((3, 2)), dma((2, 2)), dma((2, 2)),
        ],
        compiler_params=pltpu.CompilerParams(
            collective_id=0, has_side_effects=True, vmem_limit_bytes=40 * 1024 * 1024
        ),
        name="sweeps",
    )(table, start_field, source, mean_field, kl_fields)
    first_slot = lax.axis_index("mode") * local
    own_diag = lax.dynamic_slice_in_dim(diag, first_slot, local)[:, 0]
    scaling = own_diag[:, None, None, None] * totals[None]
    middle = start_field + 0.8 * (source - a_first) / scaling
    residual = source - a_second
    return middle + 0.8 * residual / scaling, residual


def solution(mesh):
    return jax.shard_map(
        functools.partial(body, mesh.shape["space"]),
        mesh=mesh,
        in_specs=(
            P("mode", "space", None, None),
            P("mode", "space", None, None),
            P("space", None, None),
            P(None, "space", None, None),
            P(),
            P(),
        ),
        out_specs=(P("mode", "space", None, None), P("mode", "space", None, None)),
        check_vma=False,
    )
```

```python
import functools

import jax
import jax.numpy as jnp
from jax import lax
from jax.experimental import pallas as pl
from jax.experimental.pallas import tpu as pltpu
from jax.sharding import PartitionSpec as P

MESH = pl.DeviceIdType.MESH
FACES = 6


def round_up(value, multiple):
    return -(-value // multiple) * multiple


def kernel(
    groups, count, triples, coef, start, source, mean, kl,
    a_first, a_second, total_out, diag_out,
    triples_here, coef_here, coefs, weights, in_first, in_second, out_first, out_second, vt, cmat,
    trade_send, trade_recv, own_sem, fetch_sem, plane_send, plane_recv, row_send, row_recv,
):
    local, planes, height, lanes = start.shape
    slots = local * groups
    rows = height // groups
    nfields = kl.shape[0] + 1
    padded = vt.shape[3]
    entries = weights.shape[0] // (planes * height)
    stride = planes * rows
    me = lax.axis_index("mode")
    at = lax.axis_index("space")
    has_left = at > 0
    has_right = at < count - 1

    barrier = pltpu.get_barrier_semaphore()
    for d in range(1, groups):
        pl.semaphore_signal(
            barrier, inc=1, device_id={"mode": lax.rem(me + d, groups)}, device_id_type=MESH
        )

    @pl.when(has_left)
    def _():
        pl.semaphore_signal(barrier, inc=1, device_id={"space": at - 1}, device_id_type=MESH)

    @pl.when(has_right)
    def _():
        pl.semaphore_signal(barrier, inc=1, device_id={"space": at + 1}, device_id_type=MESH)

    fetches = [
        pltpu.make_async_copy(triples, triples_here, fetch_sem.at[0]),
        pltpu.make_async_copy(coef, coef_here, fetch_sem.at[1]),
        pltpu.make_async_copy(mean, coefs.at[pl.ds(1, planes), 0], fetch_sem.at[2]),
    ] + [
        pltpu.make_async_copy(
            kl.at[:, z], coefs.at[z + 1, pl.ds(1, nfields - 1)], fetch_sem.at[3 + z]
        )
        for z in range(planes)
    ]
    for copy in fetches:
        copy.start()

    @pl.when(jnp.logical_not(has_left))
    def _():
        coefs[0] = jnp.zeros(coefs.shape[1:], jnp.float32)
        for k in range(2):
            vt[k, 0] = jnp.zeros(vt.shape[2:], jnp.float32)

    @pl.when(jnp.logical_not(has_right))
    def _():
        coefs[planes + 1] = jnp.zeros(coefs.shape[1:], jnp.float32)
        for k in range(2):
            vt[k, planes + 1] = jnp.zeros(vt.shape[2:], jnp.float32)

    @pl.when(me == 0)
    def _():
        for k in range(2):
            for z in range(planes):
                vt[k, z + 1, 0] = jnp.zeros(vt.shape[3:], jnp.float32)

    @pl.when(me == groups - 1)
    def _():
        for k in range(2):
            for z in range(planes):
                vt[k, z + 1, rows + 1] = jnp.zeros(vt.shape[3:], jnp.float32)

    far = lax.rem(at, 2)
    near = 1 - far

    def plane_of(side, i):
        return side * (planes - 1) + (1 - 2 * side) * i

    def band(ref, which):
        return ref.at[:, :, pl.ds(pl.multiple_of(which * rows, rows), rows), :]

    def modes(ref, which):
        size = local * stride
        return ref.at[pl.ds(pl.multiple_of(which * size, size), size), :].reshape(
            local, planes, rows, lanes
        )

    def ends(phase, target, owner):
        if phase == 0:
            return band(start, target), modes(in_first, owner)
        if phase == 1:
            return band(source, target), modes(in_second, owner)
        if phase == 2:
            return modes(out_first, target), band(a_first, owner)
        z = plane_of(near, phase - 3)
        return modes(out_second, target).at[:, z], band(a_second, owner).at[:, z]

    def remote(phase, d):
        peer = lax.rem(me + d, groups)
        src, dst = ends(phase, peer, me)
        return pltpu.make_async_remote_copy(
            src_ref=src, dst_ref=dst,
            send_sem=trade_send.at[phase, d - 1], recv_sem=trade_recv.at[phase, d - 1],
            device_id={"mode": peer}, device_id_type=MESH,
        )

    def own(phase):
        src, dst = ends(phase, me, me)
        return pltpu.make_async_copy(src, dst, own_sem.at[phase])

    def trade_start(phase, after=None):
        for d in range(1, groups):
            if after is not None:
                remote(after, d).wait_send()
            remote(phase, d).start()
        own(phase).start()

    def trade_wait_send(phase):
        for d in range(1, groups):
            remote(phase, d).wait_send()

    def trade_wait_recv(phase):
        for d in range(1, groups):
            remote(phase, d).wait_recv()
        own(phase).wait()

    def plane_copy(k, side):
        src, dst = 1 + side * (planes - 1), (planes + 1) * (1 - side)
        inner = (lambda z: coefs.at[z]) if k == 2 else (lambda z: vt.at[k, z, pl.ds(1, rows)])
        return pltpu.make_async_remote_copy(
            src_ref=inner(src), dst_ref=inner(dst),
            send_sem=plane_send.at[k, side], recv_sem=plane_recv.at[k, side],
            device_id={"space": at - 1 + 2 * side}, device_id_type=MESH,
        )

    def has(side):
        other = at - 1 + 2 * side
        return jnp.logical_and(other >= 0, other < count)

    def plane_start(k, side):
        @pl.when(has(side))
        def _():
            plane_copy(k, side).start()

    def plane_wait_send(k):
        for side in range(2):
            @pl.when(has(side))
            def _():
                plane_copy(k, side).wait_send()

    def plane_wait_recv(k, side):
        @pl.when(has(side))
        def _():
            plane_copy(k, 1 - side).wait_recv()

    has_up = me > 0
    has_down = me < groups - 1

    def row_copy(k, side):
        src, dst = (1, rows + 1) if side == 0 else (rows, 0)
        return pltpu.make_async_remote_copy(
            src_ref=vt.at[k, pl.ds(1, planes), src], dst_ref=vt.at[k, pl.ds(1, planes), dst],
            send_sem=row_send.at[k, side], recv_sem=row_recv.at[k, side],
            device_id={"mode": me - 1 if side == 0 else me + 1}, device_id_type=MESH,
        )

    def row_start(k):
        for side, sends in ((0, has_up), (1, has_down)):
            @pl.when(sends)
            def _():
                row_copy(k, side).start()

    def row_wait(k):
        for side, sends, gets in ((0, has_up, has_down), (1, has_down, has_up)):
            @pl.when(sends)
            def _():
                row_copy(k, side).wait_send()

            @pl.when(gets)
            def _():
                row_copy(k, side).wait_recv()

    pl.semaphore_wait(
        barrier, groups - 1 + has_left.astype(jnp.int32) + has_right.astype(jnp.int32)
    )
    trade_start(0)
    for copy in fetches:
        copy.wait()
    plane_start(2, 0)
    plane_start(2, 1)

    nnz = coef_here.shape[1]
    width = cmat.shape[1]
    fields_row, rows_row, cols_row = (triples_here[i:i + 1, :] for i in range(3))
    coef_row = coef_here[...]
    row_hot = lax.broadcasted_iota(jnp.int32, (padded, nnz), 0) == rows_row
    key_hot = lax.broadcasted_iota(jnp.int32, (width, nnz), 0) == fields_row * padded + cols_row
    coef_high = coef_row.astype(jnp.bfloat16).astype(jnp.float32)
    row_one = jnp.where(row_hot, 1.0, 0.0).astype(jnp.bfloat16)
    for piece, value in enumerate((coef_high, coef_row - coef_high)):
        spread = jnp.where(key_hot, value, 0.0).astype(jnp.bfloat16)
        part = lax.dot_general(
            row_one, spread, (((1,), (1,)), ((), ())), preferred_element_type=jnp.float32
        )
        cmat[piece * padded:(piece + 1) * padded, :] = part.astype(jnp.bfloat16)
    diag = jnp.sum(
        jnp.where(jnp.logical_and(row_hot, fields_row == 0), coef_row, 0.0), axis=1, keepdims=True
    )
    real = lax.broadcasted_iota(jnp.int32, (padded, 1), 0) < slots
    diag = jnp.where(real, diag, 1.0)
    diag_out[...] = jnp.broadcast_to(diag, diag_out.shape)
    step = 0.8 / diag

    plane_wait_recv(2, 0)
    plane_wait_recv(2, 1)
    lane = lax.broadcasted_iota(jnp.int32, (height, lanes), 1)
    row = lax.broadcasted_iota(jnp.int32, (height, lanes), 0)
    for z in range(planes):
        for m in range(nfields):
            c = coefs[z + 1, m]
            faces = []
            for axis, size, ids in ((1, lanes, lane), (0, height, row)):
                for shift, edge in ((size - 1, size - 1), (1, 0)):
                    other = jnp.where(ids == edge, 0.0, pltpu.roll(c, shift, axis))
                    faces.append(0.5 * (c + other))
            faces.append(0.5 * (c + coefs[z + 2, m]))
            faces.append(0.5 * (c + coefs[z, m]))
            total = functools.reduce(lambda a, b: a + b, faces)
            faces[0] = jnp.where(lane == lanes - 1, 0.0, faces[0])
            faces[1] = jnp.where(lane == 0, 0.0, faces[1])
            first = z * height * entries
            for f, value in enumerate(faces + [total]):
                weights[pl.ds(first + f * nfields + m, height, stride=entries), :] = value
            if m == 0:
                total_out[z] = total
                weights[pl.ds(first + (FACES + 1) * nfields, height, stride=entries), :] = 1.0 / total

    trade_start(1, after=0)
    trade_wait_recv(0)

    fill = jnp.zeros((padded - slots, lanes), jnp.float32)
    half = rows // 2

    def fetch(ref, z, y):
        return ref[pl.ds(z * rows + y, slots, stride=stride), :]

    def spread_weights(z, y):
        base = pl.multiple_of((z * height + me * rows + y) * entries, 8)
        return weights[pl.ds(base, entries), :]

    def fill_field(k, one_row, between):
        def edges(z, carry):
            one_row(z, 0)
            one_row(z, rows - 1)
            return carry
        lax.fori_loop(0, planes, edges, 0)
        row_start(k)
        between()
        for i in range(planes):
            z = plane_of(far, i)

            def inner(y, carry):
                one_row(z, y)
                return carry
            lax.fori_loop(1, rows - 1, inner, 0)
            if i == 0:
                plane_start(k, far)
            if i == planes - 1:
                plane_start(k, near)

    def relay(z, y):
        vt[0, z + 1, y + 1] = jnp.concatenate([fetch(in_first, z, y), fill], axis=0)

    fill_field(0, relay, lambda: None)

    def applied(k, z, y):
        w = spread_weights(z, y)
        centre = vt[k, z + 1, y + 1]
        others = (
            pltpu.roll(centre, lanes - 1, 1), pltpu.roll(centre, 1, 1),
            vt[k, z + 1, y + 2], vt[k, z + 1, y],
            vt[k, z + 2, y + 1], vt[k, z, y + 1],
        )
        parts = []
        for m in range(nfields):
            at_total = FACES * nfields + m
            value = w[at_total:at_total + 1] * centre
            for f in range(FACES):
                at_face = f * nfields + m
                value = value - w[at_face:at_face + 1] * others[f]
            parts.append(value)
        if width > nfields * padded:
            parts.append(jnp.zeros((width - nfields * padded, lanes), jnp.float32))
        return jnp.concatenate(parts, axis=0)

    def sweep(k, out, done):
        row_wait(k)
        for i in range(planes):
            z = plane_of(near, i)
            if i == 0:
                plane_wait_recv(k, near)
            if i == planes - 1:
                plane_wait_recv(k, far)

            def pair(t, carry):
                y = 2 * t
                x = jnp.concatenate([applied(k, z, y), applied(k, z, y + 1)], axis=1)
                high = x.astype(jnp.bfloat16)
                low = (x - high.astype(jnp.float32)).astype(jnp.bfloat16)
                both = jnp.dot(cmat[...], high, preferred_element_type=jnp.float32)
                rest = jnp.dot(cmat[:padded, :], low, preferred_element_type=jnp.float32)
                value = both[:padded] + (both[padded:] + rest)
                for j in range(2):
                    out[pl.ds(z * rows + y + j, slots, stride=stride), :] = value[
                        :slots, j * lanes:(j + 1) * lanes
                    ]
                return carry
            lax.fori_loop(0, half, pair, 0)
            done(i, z)

    sweep(0, out_first, lambda i, z: None)
    trade_wait_recv(1)

    def update(z, y):
        inverse = spread_weights(z, y)[(FACES + 1) * nfields:(FACES + 1) * nfields + 1]
        first = fetch(in_second, z, y) - fetch(out_first, z, y)
        first = jnp.concatenate([first, fill], axis=0)
        vt[1, z + 1, y + 1] = vt[0, z + 1, y + 1] + first * (step * inverse)

    fill_field(1, update, lambda: trade_start(2))
    sweep(1, out_second, lambda i, z: trade_start(3 + i))
    for k in range(3):
        plane_wait_send(k)
    for phase in range(1, 3 + planes):
        trade_wait_send(phase)
        if phase > 1:
            trade_wait_recv(phase)


def body(count, start_field, source, mean_field, kl_fields, triples, coef):
    local, planes, height, lanes = start_field.shape
    groups = lax.axis_size("mode")
    slots = local * groups
    nfields = kl_fields.shape[0] + 1
    rows = height // groups
    padded = round_up(slots, 8)
    width = round_up(nfields * padded, 16)
    entries = round_up((FACES + 1) * nfields + 1, 8)
    nnz = triples.shape[0]
    f32 = jnp.float32
    whole = jax.ShapeDtypeStruct(start_field.shape, f32)
    in_vmem = pl.BlockSpec(memory_space=pltpu.VMEM)
    anywhere = pl.BlockSpec(memory_space=pl.ANY)
    dma = pltpu.SemaphoreType.DMA
    a_first, a_second, totals, diag = pl.pallas_call(
        functools.partial(kernel, groups, count),
        out_shape=(
            whole, whole,
            jax.ShapeDtypeStruct((planes, height, lanes), f32),
            jax.ShapeDtypeStruct((padded, lanes), f32),
        ),
        in_specs=[pl.BlockSpec(memory_space=pltpu.HBM)] * 6,
        out_specs=(anywhere, anywhere, in_vmem, in_vmem),
        scratch_shapes=[
            pltpu.VMEM((3, nnz), jnp.int32),
            pltpu.VMEM((1, nnz), f32),
            pltpu.VMEM((planes + 2, nfields, height, lanes), f32),
            pltpu.VMEM((planes * height * entries, lanes), f32),
            pltpu.VMEM((slots * planes * rows, lanes), f32),
            pltpu.VMEM((slots * planes * rows, lanes), f32),
            pltpu.VMEM((slots * planes * rows, lanes), f32),
            pltpu.VMEM((slots * planes * rows, lanes), f32),
            pltpu.VMEM((2, planes + 2, rows + 2, padded, lanes), f32),
            pltpu.VMEM((2 * padded, width), jnp.bfloat16),
            dma((3 + planes, groups - 1)), dma((3 + planes, groups - 1)), dma((3 + planes,)),
            dma((3 + planes,)),
            dma((3, 2)), dma((3, 2)), dma((2, 2)), dma((2, 2)),
        ],
        compiler_params=pltpu.CompilerParams(
            collective_id=0, has_side_effects=True, vmem_limit_bytes=62 * 1024 * 1024
        ),
        name="sweeps",
    )(triples.T, coef[None], start_field, source, mean_field, kl_fields)
    first_slot = lax.axis_index("mode") * local
    own_diag = lax.dynamic_slice_in_dim(diag, first_slot, local)[:, 0]
    scaling = own_diag[:, None, None, None] * totals[None]
    middle = start_field + 0.8 * (source - a_first) / scaling
    residual = source - a_second
    return middle + 0.8 * residual / scaling, residual


def solution(mesh):
    return jax.shard_map(
        functools.partial(body, mesh.shape["space"]),
        mesh=mesh,
        in_specs=(
            P("mode", "space", None, None),
            P("mode", "space", None, None),
            P("space", None, None),
            P(None, "space", None, None),
            P(),
            P(),
        ),
        out_specs=(P("mode", "space", None, None), P("mode", "space", None, None)),
        check_vma=False,
    )
```

```python
import functools

import jax
import jax.numpy as jnp
from jax import lax
from jax.experimental import pallas as pl
from jax.experimental.pallas import tpu as pltpu
from jax.sharding import PartitionSpec as P

MESH = pl.DeviceIdType.MESH
FACES = 6


def round_up(value, multiple):
    return -(-value // multiple) * multiple


def kernel(
    groups, count, triples, coef, start, source, mean, kl,
    a_first, a_second, total_out, diag_out,
    triples_here, coef_here, coefs, weights, in_first, in_second, out_first, out_second, vt, cmat,
    trade_send, trade_recv, own_sem, fetch_sem, plane_send, plane_recv, row_send, row_recv,
):
    local, planes, height, lanes = start.shape
    slots = local * groups
    rows = height // groups
    nfields = kl.shape[0] + 1
    padded = vt.shape[3]
    entries = weights.shape[0] // (planes * height)
    stride = planes * rows
    me = lax.axis_index("mode")
    at = lax.axis_index("space")
    has_left = at > 0
    has_right = at < count - 1

    barrier = pltpu.get_barrier_semaphore()
    for d in range(1, groups):
        pl.semaphore_signal(
            barrier, inc=1, device_id={"mode": lax.rem(me + d, groups)}, device_id_type=MESH
        )

    @pl.when(has_left)
    def _():
        pl.semaphore_signal(barrier, inc=1, device_id={"space": at - 1}, device_id_type=MESH)

    @pl.when(has_right)
    def _():
        pl.semaphore_signal(barrier, inc=1, device_id={"space": at + 1}, device_id_type=MESH)

    fetches = [
        pltpu.make_async_copy(triples, triples_here, fetch_sem.at[0]),
        pltpu.make_async_copy(coef, coef_here, fetch_sem.at[1]),
        pltpu.make_async_copy(mean, coefs.at[pl.ds(1, planes), 0], fetch_sem.at[2]),
    ] + [
        pltpu.make_async_copy(
            kl.at[:, z], coefs.at[z + 1, pl.ds(1, nfields - 1)], fetch_sem.at[3 + z]
        )
        for z in range(planes)
    ]
    for copy in fetches:
        copy.start()

    @pl.when(jnp.logical_not(has_left))
    def _():
        coefs[0] = jnp.zeros(coefs.shape[1:], jnp.float32)
        for k in range(2):
            vt[k, 0] = jnp.zeros(vt.shape[2:], jnp.float32)

    @pl.when(jnp.logical_not(has_right))
    def _():
        coefs[planes + 1] = jnp.zeros(coefs.shape[1:], jnp.float32)
        for k in range(2):
            vt[k, planes + 1] = jnp.zeros(vt.shape[2:], jnp.float32)

    @pl.when(me == 0)
    def _():
        for k in range(2):
            for z in range(planes):
                vt[k, z + 1, 0] = jnp.zeros(vt.shape[3:], jnp.float32)

    @pl.when(me == groups - 1)
    def _():
        for k in range(2):
            for z in range(planes):
                vt[k, z + 1, rows + 1] = jnp.zeros(vt.shape[3:], jnp.float32)

    far = lax.rem(at, 2)
    near = 1 - far

    def plane_of(side, i):
        return side * (planes - 1) + (1 - 2 * side) * i

    def band(ref, which):
        return ref.at[:, :, pl.ds(pl.multiple_of(which * rows, rows), rows), :]

    def modes(ref, which):
        size = local * stride
        return ref.at[pl.ds(pl.multiple_of(which * size, size), size), :].reshape(
            local, planes, rows, lanes
        )

    def ends(phase, i, target, owner):
        if phase < 2:
            z = plane_of(far, i)
            return (
                band((start, source)[phase], target).at[:, z],
                modes((in_first, in_second)[phase], owner).at[:, z],
            )
        z = plane_of(near, i)
        return (
            modes((out_first, out_second)[phase - 2], target).at[:, z],
            band((a_first, a_second)[phase - 2], owner).at[:, z],
        )

    def remote(phase, i, d):
        peer = lax.rem(me + d, groups)
        src, dst = ends(phase, i, peer, me)
        part = phase * planes + i
        return pltpu.make_async_remote_copy(
            src_ref=src, dst_ref=dst,
            send_sem=trade_send.at[part, d - 1], recv_sem=trade_recv.at[part, d - 1],
            device_id={"mode": peer}, device_id_type=MESH,
        )

    def own(phase, i):
        src, dst = ends(phase, i, me, me)
        return pltpu.make_async_copy(src, dst, own_sem.at[phase * planes + i])

    def trade_start(phase, i, after=None):
        for d in range(1, groups):
            if after is not None:
                remote(*after, d).wait_send()
            remote(phase, i, d).start()
        own(phase, i).start()

    def trade_wait_send(phase, i):
        for d in range(1, groups):
            remote(phase, i, d).wait_send()

    def trade_wait_recv(phase, i):
        for d in range(1, groups):
            remote(phase, i, d).wait_recv()
        own(phase, i).wait()

    def plane_copy(k, side):
        src, dst = 1 + side * (planes - 1), (planes + 1) * (1 - side)
        inner = (lambda z: coefs.at[z]) if k == 2 else (lambda z: vt.at[k, z, pl.ds(1, rows)])
        return pltpu.make_async_remote_copy(
            src_ref=inner(src), dst_ref=inner(dst),
            send_sem=plane_send.at[k, side], recv_sem=plane_recv.at[k, side],
            device_id={"space": at - 1 + 2 * side}, device_id_type=MESH,
        )

    def has(side):
        other = at - 1 + 2 * side
        return jnp.logical_and(other >= 0, other < count)

    def plane_start(k, side):
        @pl.when(has(side))
        def _():
            plane_copy(k, side).start()

    def plane_wait_send(k):
        for side in range(2):
            @pl.when(has(side))
            def _():
                plane_copy(k, side).wait_send()

    def plane_wait_recv(k, side):
        @pl.when(has(side))
        def _():
            plane_copy(k, 1 - side).wait_recv()

    has_up = me > 0
    has_down = me < groups - 1

    def row_copy(k, z, side):
        src, dst = (1, rows + 1) if side == 0 else (rows, 0)
        return pltpu.make_async_remote_copy(
            src_ref=vt.at[k, z + 1, src], dst_ref=vt.at[k, z + 1, dst],
            send_sem=row_send.at[k, z, side], recv_sem=row_recv.at[k, z, side],
            device_id={"mode": me - 1 if side == 0 else me + 1}, device_id_type=MESH,
        )

    def row_start(k, z):
        for side, sends in ((0, has_up), (1, has_down)):
            @pl.when(sends)
            def _():
                row_copy(k, z, side).start()

    def row_wait_send(k, z):
        for side, sends in ((0, has_up), (1, has_down)):
            @pl.when(sends)
            def _():
                row_copy(k, z, side).wait_send()

    def row_wait_recv(k, z):
        for side, gets in ((0, has_down), (1, has_up)):
            @pl.when(gets)
            def _():
                row_copy(k, z, side).wait_recv()

    pl.semaphore_wait(
        barrier, groups - 1 + has_left.astype(jnp.int32) + has_right.astype(jnp.int32)
    )
    trade_start(0, 0)
    for copy in fetches:
        copy.wait()
    plane_start(2, 0)
    plane_start(2, 1)

    nnz = coef_here.shape[1]
    width = cmat.shape[1]
    fields_row, rows_row, cols_row = (triples_here[i:i + 1, :] for i in range(3))
    coef_row = coef_here[...]
    row_hot = lax.broadcasted_iota(jnp.int32, (padded, nnz), 0) == rows_row
    key_hot = lax.broadcasted_iota(jnp.int32, (width, nnz), 0) == fields_row * padded + cols_row
    coef_high = coef_row.astype(jnp.bfloat16).astype(jnp.float32)
    row_one = jnp.where(row_hot, 1.0, 0.0).astype(jnp.bfloat16)
    for piece, value in enumerate((coef_high, coef_row - coef_high)):
        spread = jnp.where(key_hot, value, 0.0).astype(jnp.bfloat16)
        part = lax.dot_general(
            row_one, spread, (((1,), (1,)), ((), ())), preferred_element_type=jnp.float32
        )
        cmat[piece * padded:(piece + 1) * padded, :] = part.astype(jnp.bfloat16)
    diag = jnp.sum(
        jnp.where(jnp.logical_and(row_hot, fields_row == 0), coef_row, 0.0), axis=1, keepdims=True
    )
    real = lax.broadcasted_iota(jnp.int32, (padded, 1), 0) < slots
    diag = jnp.where(real, diag, 1.0)
    own_hot = lax.broadcasted_iota(jnp.int32, (diag_out.shape[0], nnz), 0) + me * local == rows_row
    own_diag = jnp.sum(
        jnp.where(jnp.logical_and(own_hot, fields_row == 0), coef_row, 0.0), axis=1, keepdims=True
    )
    diag_out[...] = jnp.broadcast_to(own_diag, diag_out.shape)
    step = 0.8 / diag

    fill = jnp.zeros((padded - slots, lanes), jnp.float32)

    def fetch(ref, z, y):
        return ref[pl.ds(z * rows + y, slots, stride=stride), :]

    def spread_weights(z, y):
        base = pl.multiple_of((z * height + me * rows + y) * entries, 8)
        return weights[pl.ds(base, entries), :]

    def fill_plane(k, i, one_row):
        z = plane_of(far, i)
        one_row(z, 0)
        one_row(z, rows - 1)
        row_start(k, z)

        def inner(y, carry):
            one_row(z, y)
            return carry
        lax.fori_loop(1, rows - 1, inner, 0)
        if i == 0:
            plane_start(k, far)
        if i == planes - 1:
            plane_start(k, near)

    def relay(z, y):
        vt[0, z + 1, y + 1] = jnp.concatenate([fetch(in_first, z, y), fill], axis=0)

    for i in range(planes - 1):
        trade_start(0, i + 1, after=(0, i))
        trade_wait_recv(0, i)
        fill_plane(0, i, relay)

    plane_wait_recv(2, 0)
    plane_wait_recv(2, 1)
    lane = lax.broadcasted_iota(jnp.int32, (height, lanes), 1)
    row = lax.broadcasted_iota(jnp.int32, (height, lanes), 0)
    for z in range(planes):
        for m in range(nfields):
            c = coefs[z + 1, m]
            faces = []
            for axis, size, ids in ((1, lanes, lane), (0, height, row)):
                for shift, edge in ((size - 1, size - 1), (1, 0)):
                    other = jnp.where(ids == edge, 0.0, pltpu.roll(c, shift, axis))
                    faces.append(0.5 * (c + other))
            faces.append(0.5 * (c + coefs[z + 2, m]))
            faces.append(0.5 * (c + coefs[z, m]))
            total = functools.reduce(lambda a, b: a + b, faces)
            faces[0] = jnp.where(lane == lanes - 1, 0.0, faces[0])
            faces[1] = jnp.where(lane == 0, 0.0, faces[1])
            first = z * height * entries
            for f, value in enumerate(faces + [total]):
                weights[pl.ds(first + f * nfields + m, height, stride=entries), :] = value
            if m == 0:
                total_out[z] = total
                weights[pl.ds(first + (FACES + 1) * nfields, height, stride=entries), :] = 1.0 / total

    last = planes - 1
    trade_start(1, 0, after=(0, last))
    trade_wait_recv(0, last)
    fill_plane(0, last, relay)

    def applied(k, z, y):
        w = spread_weights(z, y)
        centre = vt[k, z + 1, y + 1]
        others = (
            pltpu.roll(centre, lanes - 1, 1), pltpu.roll(centre, 1, 1),
            vt[k, z + 1, y + 2], vt[k, z + 1, y],
            vt[k, z + 2, y + 1], vt[k, z, y + 1],
        )
        parts = []
        for m in range(nfields):
            at_total = FACES * nfields + m
            value = w[at_total:at_total + 1] * centre
            for f in range(FACES):
                at_face = f * nfields + m
                value = value - w[at_face:at_face + 1] * others[f]
            parts.append(value)
        if width > nfields * padded:
            parts.append(jnp.zeros((width - nfields * padded, lanes), jnp.float32))
        return jnp.concatenate(parts, axis=0)

    def product(k, z, y):
        x = jnp.concatenate([applied(k, z, y), applied(k, z, y + 1)], axis=1)
        high = x.astype(jnp.bfloat16)
        low = (x - high.astype(jnp.float32)).astype(jnp.bfloat16)
        both = jnp.dot(cmat[...], high, preferred_element_type=jnp.float32)
        rest = jnp.dot(cmat[:padded, :], low, preferred_element_type=jnp.float32)
        return both[:padded] + (both[padded:] + rest)

    def sweep(k, i, out):
        z = plane_of(near, i)
        row_wait_recv(k, z)
        if i == 0:
            plane_wait_recv(k, near)
        if i == last:
            plane_wait_recv(k, far)

        def group(t, carry):
            y = 4 * t
            values = [product(k, z, y), product(k, z, y + 2)]
            for j in range(4):
                out[pl.ds(z * rows + y + j, slots, stride=stride), :] = values[j // 2][
                    :slots, (j % 2) * lanes:(j % 2 + 1) * lanes
                ]
            return carry
        lax.fori_loop(0, rows // 4, group, 0)

    for i in range(planes):
        sweep(0, i, out_first)
        if i < last:
            trade_start(1, i + 1, after=(1, i))

    def update(z, y):
        inverse = spread_weights(z, y)[(FACES + 1) * nfields:(FACES + 1) * nfields + 1]
        first = fetch(in_second, z, y) - fetch(out_first, z, y)
        first = jnp.concatenate([first, fill], axis=0)
        vt[1, z + 1, y + 1] = vt[0, z + 1, y + 1] + first * (step * inverse)

    for i in range(planes):
        if i == last:
            trade_start(2, 0, after=(1, last))
        trade_wait_recv(1, i)
        fill_plane(1, i, update)
    for i in range(1, planes):
        trade_start(2, i)
    for i in range(planes):
        sweep(1, i, out_second)
        trade_start(3, i)
    for k in range(3):
        plane_wait_send(k)
        if k < 2:
            for z in range(planes):
                row_wait_send(k, z)
    for phase in (2, 3):
        for i in range(planes):
            trade_wait_send(phase, i)
            trade_wait_recv(phase, i)


def body(count, start_field, source, mean_field, kl_fields, triples, coef):
    local, planes, height, lanes = start_field.shape
    groups = lax.axis_size("mode")
    slots = local * groups
    nfields = kl_fields.shape[0] + 1
    rows = height // groups
    padded = round_up(slots, 8)
    width = round_up(nfields * padded, 16)
    entries = round_up((FACES + 1) * nfields + 1, 8)
    nnz = triples.shape[0]
    f32 = jnp.float32
    whole = jax.ShapeDtypeStruct(start_field.shape, f32)
    in_vmem = pl.BlockSpec(memory_space=pltpu.VMEM)
    anywhere = pl.BlockSpec(memory_space=pl.ANY)
    dma = pltpu.SemaphoreType.DMA
    a_first, a_second, totals, diag = pl.pallas_call(
        functools.partial(kernel, groups, count),
        out_shape=(
            whole, whole,
            jax.ShapeDtypeStruct((planes, height, lanes), f32),
            jax.ShapeDtypeStruct((round_up(local, 8), lanes), f32),
        ),
        in_specs=[pl.BlockSpec(memory_space=pltpu.HBM)] * 6,
        out_specs=(anywhere, anywhere, in_vmem, in_vmem),
        scratch_shapes=[
            pltpu.VMEM((3, nnz), jnp.int32),
            pltpu.VMEM((1, nnz), f32),
            pltpu.VMEM((planes + 2, nfields, height, lanes), f32),
            pltpu.VMEM((planes * height * entries, lanes), f32),
            pltpu.VMEM((slots * planes * rows, lanes), f32),
            pltpu.VMEM((slots * planes * rows, lanes), f32),
            pltpu.VMEM((slots * planes * rows, lanes), f32),
            pltpu.VMEM((slots * planes * rows, lanes), f32),
            pltpu.VMEM((2, planes + 2, rows + 2, padded, lanes), f32),
            pltpu.VMEM((2 * padded, width), jnp.bfloat16),
            dma((4 * planes, groups - 1)), dma((4 * planes, groups - 1)), dma((4 * planes,)),
            dma((3 + planes,)),
            dma((3, 2)), dma((3, 2)), dma((2, planes, 2)), dma((2, planes, 2)),
        ],
        compiler_params=pltpu.CompilerParams(
            collective_id=0, has_side_effects=True, vmem_limit_bytes=62 * 1024 * 1024
        ),
        name="sweeps",
    )(triples.T, coef[None], start_field, source, mean_field, kl_fields)
    scaling = diag[:local, None, None, :] * totals[None]
    middle = start_field + 0.8 * (source - a_first) / scaling
    residual = source - a_second
    return middle + 0.8 * residual / scaling, residual


def solution(mesh):
    return jax.shard_map(
        functools.partial(body, mesh.shape["space"]),
        mesh=mesh,
        in_specs=(
            P("mode", "space", None, None),
            P("mode", "space", None, None),
            P("space", None, None),
            P(None, "space", None, None),
            P(),
            P(),
        ),
        out_specs=(P("mode", "space", None, None), P("mode", "space", None, None)),
        check_vma=False,
    )
```

```python
import functools

import jax
import jax.numpy as jnp
from jax import lax
from jax.experimental import pallas as pl
from jax.experimental.pallas import tpu as pltpu
from jax.sharding import PartitionSpec as P

MESH = pl.DeviceIdType.MESH
FACES = 6


def round_up(value, multiple):
    return -(-value // multiple) * multiple


def kernel(
    groups, count, triples, coef, start, source, mean, kl,
    smoothed_out, residual_out,
    start_here, source_here, a_first, a_second, inverse_total, own_step,
    triples_here, coef_here, coefs, weights, in_first, in_second, out_first, out_second, vt, cmat,
    trade_send, trade_recv, own_sem, fetch_sem, home_sem, out_sem, plane_send, plane_recv, row_send, row_recv,
):
    local, planes, height, lanes = start.shape
    slots = local * groups
    rows = height // groups
    nfields = kl.shape[0] + 1
    padded = vt.shape[3]
    entries = weights.shape[0] // (planes * height)
    stride = planes * rows
    me = lax.axis_index("mode")
    at = lax.axis_index("space")
    has_left = at > 0
    has_right = at < count - 1

    barrier = pltpu.get_barrier_semaphore()
    for d in range(1, groups):
        pl.semaphore_signal(
            barrier, inc=1, device_id={"mode": lax.rem(me + d, groups)}, device_id_type=MESH
        )

    @pl.when(has_left)
    def _():
        pl.semaphore_signal(barrier, inc=1, device_id={"space": at - 1}, device_id_type=MESH)

    @pl.when(has_right)
    def _():
        pl.semaphore_signal(barrier, inc=1, device_id={"space": at + 1}, device_id_type=MESH)

    fields_here = [
        pltpu.make_async_copy(start, start_here, home_sem.at[0]),
        pltpu.make_async_copy(source, source_here, home_sem.at[1]),
    ]
    fetches = [
        pltpu.make_async_copy(triples, triples_here, fetch_sem.at[0]),
        pltpu.make_async_copy(coef, coef_here, fetch_sem.at[1]),
        pltpu.make_async_copy(mean, coefs.at[pl.ds(1, planes), 0], fetch_sem.at[2]),
    ] + [
        pltpu.make_async_copy(
            kl.at[:, z], coefs.at[z + 1, pl.ds(1, nfields - 1)], fetch_sem.at[3 + z]
        )
        for z in range(planes)
    ]
    for copy in fetches:
        copy.start()

    @pl.when(jnp.logical_not(has_left))
    def _():
        coefs[0] = jnp.zeros(coefs.shape[1:], jnp.float32)
        for k in range(2):
            vt[k, 0] = jnp.zeros(vt.shape[2:], jnp.float32)

    @pl.when(jnp.logical_not(has_right))
    def _():
        coefs[planes + 1] = jnp.zeros(coefs.shape[1:], jnp.float32)
        for k in range(2):
            vt[k, planes + 1] = jnp.zeros(vt.shape[2:], jnp.float32)

    @pl.when(me == 0)
    def _():
        for k in range(2):
            for z in range(planes):
                vt[k, z + 1, 0] = jnp.zeros(vt.shape[3:], jnp.float32)

    @pl.when(me == groups - 1)
    def _():
        for k in range(2):
            for z in range(planes):
                vt[k, z + 1, rows + 1] = jnp.zeros(vt.shape[3:], jnp.float32)

    far = lax.rem(at, 2)
    near = 1 - far

    def plane_of(side, i):
        return side * (planes - 1) + (1 - 2 * side) * i

    def band(ref, which):
        return ref.at[:, :, pl.ds(pl.multiple_of(which * rows, rows), rows), :]

    def modes(ref, which):
        size = local * stride
        return ref.at[pl.ds(pl.multiple_of(which * size, size), size), :].reshape(
            local, planes, rows, lanes
        )

    def ends(phase, i, target, owner):
        if phase < 2:
            z = plane_of(far, i)
            return (
                band((start, source)[phase], target).at[:, z],
                modes((in_first, in_second)[phase], owner).at[:, z],
            )
        z = plane_of(near, i)
        return (
            modes((out_first, out_second)[phase - 2], target).at[:, z],
            band((a_first, a_second)[phase - 2], owner).at[:, z],
        )

    def remote(phase, i, d):
        peer = lax.rem(me + d, groups)
        src, dst = ends(phase, i, peer, me)
        part = phase * planes + i
        return pltpu.make_async_remote_copy(
            src_ref=src, dst_ref=dst,
            send_sem=trade_send.at[part, d - 1], recv_sem=trade_recv.at[part, d - 1],
            device_id={"mode": peer}, device_id_type=MESH,
        )

    def own(phase, i):
        src, dst = ends(phase, i, me, me)
        return pltpu.make_async_copy(src, dst, own_sem.at[phase * planes + i])

    def trade_start(phase, i, after=None):
        for d in range(1, groups):
            if after is not None:
                remote(*after, d).wait_send()
            remote(phase, i, d).start()
        own(phase, i).start()

    def trade_wait_send(phase, i):
        for d in range(1, groups):
            remote(phase, i, d).wait_send()

    def trade_wait_recv(phase, i):
        for d in range(1, groups):
            remote(phase, i, d).wait_recv()
        own(phase, i).wait()

    def plane_copy(k, side):
        src, dst = 1 + side * (planes - 1), (planes + 1) * (1 - side)
        inner = (lambda z: coefs.at[z]) if k == 2 else (lambda z: vt.at[k, z, pl.ds(1, rows)])
        return pltpu.make_async_remote_copy(
            src_ref=inner(src), dst_ref=inner(dst),
            send_sem=plane_send.at[k, side], recv_sem=plane_recv.at[k, side],
            device_id={"space": at - 1 + 2 * side}, device_id_type=MESH,
        )

    def has(side):
        other = at - 1 + 2 * side
        return jnp.logical_and(other >= 0, other < count)

    def plane_start(k, side):
        @pl.when(has(side))
        def _():
            plane_copy(k, side).start()

    def plane_wait_send(k):
        for side in range(2):
            @pl.when(has(side))
            def _():
                plane_copy(k, side).wait_send()

    def plane_wait_recv(k, side):
        @pl.when(has(side))
        def _():
            plane_copy(k, 1 - side).wait_recv()

    has_up = me > 0
    has_down = me < groups - 1

    def row_copy(k, z, side):
        src, dst = (1, rows + 1) if side == 0 else (rows, 0)
        return pltpu.make_async_remote_copy(
            src_ref=vt.at[k, z + 1, src], dst_ref=vt.at[k, z + 1, dst],
            send_sem=row_send.at[k, z, side], recv_sem=row_recv.at[k, z, side],
            device_id={"mode": me - 1 if side == 0 else me + 1}, device_id_type=MESH,
        )

    def row_start(k, z):
        for side, sends in ((0, has_up), (1, has_down)):
            @pl.when(sends)
            def _():
                row_copy(k, z, side).start()

    def row_wait_send(k, z):
        for side, sends in ((0, has_up), (1, has_down)):
            @pl.when(sends)
            def _():
                row_copy(k, z, side).wait_send()

    def row_wait_recv(k, z):
        for side, gets in ((0, has_down), (1, has_up)):
            @pl.when(gets)
            def _():
                row_copy(k, z, side).wait_recv()

    pl.semaphore_wait(
        barrier, groups - 1 + has_left.astype(jnp.int32) + has_right.astype(jnp.int32)
    )
    trade_start(0, 0)
    for copy in fetches:
        copy.wait()
    for copy in fields_here:
        copy.start()
    plane_start(2, 0)
    plane_start(2, 1)

    nnz = coef_here.shape[1]
    width = cmat.shape[1]
    fields_row, rows_row, cols_row = (triples_here[i:i + 1, :] for i in range(3))
    coef_row = coef_here[...]
    row_hot = lax.broadcasted_iota(jnp.int32, (padded, nnz), 0) == rows_row
    key_hot = lax.broadcasted_iota(jnp.int32, (width, nnz), 0) == fields_row * padded + cols_row
    coef_high = coef_row.astype(jnp.bfloat16).astype(jnp.float32)
    row_one = jnp.where(row_hot, 1.0, 0.0).astype(jnp.bfloat16)
    for piece, value in enumerate((coef_high, coef_row - coef_high)):
        spread = jnp.where(key_hot, value, 0.0).astype(jnp.bfloat16)
        part = lax.dot_general(
            row_one, spread, (((1,), (1,)), ((), ())), preferred_element_type=jnp.float32
        )
        cmat[piece * padded:(piece + 1) * padded, :] = part.astype(jnp.bfloat16)
    diag = jnp.sum(
        jnp.where(jnp.logical_and(row_hot, fields_row == 0), coef_row, 0.0), axis=1, keepdims=True
    )
    real = lax.broadcasted_iota(jnp.int32, (padded, 1), 0) < slots
    diag = jnp.where(real, diag, 1.0)
    own_ids = lax.broadcasted_iota(jnp.int32, (own_step.shape[0], nnz), 0)
    own_diag = jnp.sum(
        jnp.where(jnp.logical_and(own_ids + me * local == rows_row, fields_row == 0), coef_row, 0.0),
        axis=1, keepdims=True,
    )
    own_diag = jnp.where(own_ids[:, :1] < local, own_diag, 1.0)
    own_step[...] = jnp.broadcast_to(0.8 / own_diag, own_step.shape)
    step = 0.8 / diag

    fill = jnp.zeros((padded - slots, lanes), jnp.float32)

    def fetch(ref, z, y):
        return ref[pl.ds(z * rows + y, slots, stride=stride), :]

    def spread_weights(z, y):
        base = pl.multiple_of((z * height + me * rows + y) * entries, 8)
        return weights[pl.ds(base, entries), :]

    def fill_plane(k, i, one_row):
        z = plane_of(far, i)
        one_row(z, 0)
        one_row(z, rows - 1)
        row_start(k, z)

        def inner(y, carry):
            one_row(z, y)
            return carry
        lax.fori_loop(1, rows - 1, inner, 0)
        if i == 0:
            plane_start(k, far)
        if i == planes - 1:
            plane_start(k, near)

    def relay(z, y):
        vt[0, z + 1, y + 1] = jnp.concatenate([fetch(in_first, z, y), fill], axis=0)

    for i in range(planes - 1):
        trade_start(0, i + 1, after=(0, i))
        trade_wait_recv(0, i)
        fill_plane(0, i, relay)

    plane_wait_recv(2, 0)
    plane_wait_recv(2, 1)
    lane = lax.broadcasted_iota(jnp.int32, (height, lanes), 1)
    row = lax.broadcasted_iota(jnp.int32, (height, lanes), 0)
    for z in range(planes):
        for m in range(nfields):
            c = coefs[z + 1, m]
            faces = []
            for axis, size, ids in ((1, lanes, lane), (0, height, row)):
                for shift, edge in ((size - 1, size - 1), (1, 0)):
                    other = jnp.where(ids == edge, 0.0, pltpu.roll(c, shift, axis))
                    faces.append(0.5 * (c + other))
            faces.append(0.5 * (c + coefs[z + 2, m]))
            faces.append(0.5 * (c + coefs[z, m]))
            total = functools.reduce(lambda a, b: a + b, faces)
            faces[0] = jnp.where(lane == lanes - 1, 0.0, faces[0])
            faces[1] = jnp.where(lane == 0, 0.0, faces[1])
            first = z * height * entries
            for f, value in enumerate(faces + [total]):
                weights[pl.ds(first + f * nfields + m, height, stride=entries), :] = value
            if m == 0:
                inverse_total[z] = 1.0 / total
                weights[pl.ds(first + (FACES + 1) * nfields, height, stride=entries), :] = (
                    inverse_total[z]
                )

    last = planes - 1
    trade_start(1, 0, after=(0, last))
    trade_wait_recv(0, last)
    fill_plane(0, last, relay)

    def applied(k, z, y):
        w = spread_weights(z, y)
        centre = vt[k, z + 1, y + 1]
        others = (
            pltpu.roll(centre, lanes - 1, 1), pltpu.roll(centre, 1, 1),
            vt[k, z + 1, y + 2], vt[k, z + 1, y],
            vt[k, z + 2, y + 1], vt[k, z, y + 1],
        )
        parts = []
        for m in range(nfields):
            at_total = FACES * nfields + m
            value = w[at_total:at_total + 1] * centre
            for f in range(FACES):
                at_face = f * nfields + m
                value = value - w[at_face:at_face + 1] * others[f]
            parts.append(value)
        if width > nfields * padded:
            parts.append(jnp.zeros((width - nfields * padded, lanes), jnp.float32))
        return jnp.concatenate(parts, axis=0)

    def product(k, z, y):
        x = jnp.concatenate([applied(k, z, y), applied(k, z, y + 1)], axis=1)
        high = x.astype(jnp.bfloat16)
        low = (x - high.astype(jnp.float32)).astype(jnp.bfloat16)
        both = jnp.dot(cmat[...], high, preferred_element_type=jnp.float32)
        rest = jnp.dot(cmat[:padded, :], low, preferred_element_type=jnp.float32)
        return both[:padded] + (both[padded:] + rest)

    def sweep(k, i, out):
        z = plane_of(near, i)
        row_wait_recv(k, z)
        if i == 0:
            plane_wait_recv(k, near)
        if i == last:
            plane_wait_recv(k, far)

        def group(t, carry):
            y = 4 * t
            values = [product(k, z, y), product(k, z, y + 2)]
            for j in range(4):
                out[pl.ds(z * rows + y + j, slots, stride=stride), :] = values[j // 2][
                    :slots, (j % 2) * lanes:(j % 2 + 1) * lanes
                ]
            return carry
        lax.fori_loop(0, rows // 4, group, 0)

    for i in range(planes):
        sweep(0, i, out_first)
        if i < last:
            trade_start(1, i + 1, after=(1, i))

    def update(z, y):
        inverse = spread_weights(z, y)[(FACES + 1) * nfields:(FACES + 1) * nfields + 1]
        first = fetch(in_second, z, y) - fetch(out_first, z, y)
        first = jnp.concatenate([first, fill], axis=0)
        vt[1, z + 1, y + 1] = vt[0, z + 1, y + 1] + first * (step * inverse)

    for i in range(planes):
        if i == last:
            trade_start(2, 0, after=(1, last))
        trade_wait_recv(1, i)
        fill_plane(1, i, update)
    for i in range(1, planes):
        trade_start(2, i)
    for i in range(planes):
        sweep(1, i, out_second)
        trade_start(3, i)

    for copy in fields_here:
        copy.wait()
    for i in range(planes):
        trade_wait_recv(2, i)

    def make_middle(j, carry):
        gain = own_step[pl.ds(j, 1), :]
        for z in range(planes):
            first = source_here[j, z] - a_first[j, z]
            start_here[j, z] = start_here[j, z] + first * (gain * inverse_total[z])
        return carry
    lax.fori_loop(0, local, make_middle, 0)

    def results(i):
        z = plane_of(near, i)
        return [
            pltpu.make_async_copy(held.at[:, z], out.at[:, z], out_sem.at[i, n])
            for n, (held, out) in enumerate(((start_here, smoothed_out), (a_second, residual_out)))
        ]

    for i in range(planes):
        z = plane_of(near, i)
        trade_wait_recv(3, i)

        def make_outputs(j, carry):
            residual = source_here[j, z] - a_second[j, z]
            a_second[j, z] = residual
            gain = own_step[pl.ds(j, 1), :] * inverse_total[z]
            start_here[j, z] = start_here[j, z] + residual * gain
            return carry
        lax.fori_loop(0, local, make_outputs, 0)
        for copy in results(i):
            copy.start()
    for k in range(3):
        plane_wait_send(k)
        if k < 2:
            for z in range(planes):
                row_wait_send(k, z)
    for phase in (2, 3):
        for i in range(planes):
            trade_wait_send(phase, i)
    for i in range(planes):
        for copy in results(i):
            copy.wait()


def body(count, start_field, source, mean_field, kl_fields, triples, coef):
    local, planes, height, lanes = start_field.shape
    groups = lax.axis_size("mode")
    slots = local * groups
    nfields = kl_fields.shape[0] + 1
    rows = height // groups
    padded = round_up(slots, 8)
    width = round_up(nfields * padded, 16)
    entries = round_up((FACES + 1) * nfields + 1, 8)
    nnz = triples.shape[0]
    f32 = jnp.float32
    whole = jax.ShapeDtypeStruct(start_field.shape, f32)
    anywhere = pl.BlockSpec(memory_space=pl.ANY)
    dma = pltpu.SemaphoreType.DMA
    smoothed, residual = pl.pallas_call(
        functools.partial(kernel, groups, count),
        out_shape=(whole, whole),
        in_specs=[pl.BlockSpec(memory_space=pltpu.HBM)] * 6,
        out_specs=(anywhere, anywhere),
        scratch_shapes=[
            *[pltpu.VMEM(start_field.shape, f32)] * 4,
            pltpu.VMEM((planes, height, lanes), f32),
            pltpu.VMEM((round_up(local, 8), lanes), f32),
            pltpu.VMEM((3, nnz), jnp.int32),
            pltpu.VMEM((1, nnz), f32),
            pltpu.VMEM((planes + 2, nfields, height, lanes), f32),
            pltpu.VMEM((planes * height * entries, lanes), f32),
            pltpu.VMEM((slots * planes * rows, lanes), f32),
            pltpu.VMEM((slots * planes * rows, lanes), f32),
            pltpu.VMEM((slots * planes * rows, lanes), f32),
            pltpu.VMEM((slots * planes * rows, lanes), f32),
            pltpu.VMEM((2, planes + 2, rows + 2, padded, lanes), f32),
            pltpu.VMEM((2 * padded, width), jnp.bfloat16),
            dma((4 * planes, groups - 1)), dma((4 * planes, groups - 1)), dma((4 * planes,)),
            dma((3 + planes,)), dma((2,)), dma((planes, 2)),
            dma((3, 2)), dma((3, 2)), dma((2, planes, 2)), dma((2, planes, 2)),
        ],
        compiler_params=pltpu.CompilerParams(
            collective_id=0, has_side_effects=True, vmem_limit_bytes=62 * 1024 * 1024
        ),
        name="sweeps",
    )(triples.T, coef[None], start_field, source, mean_field, kl_fields)
    return smoothed, residual


def solution(mesh):
    return jax.shard_map(
        functools.partial(body, mesh.shape["space"]),
        mesh=mesh,
        in_specs=(
            P("mode", "space", None, None),
            P("mode", "space", None, None),
            P("space", None, None),
            P(None, "space", None, None),
            P(),
            P(),
        ),
        out_specs=(P("mode", "space", None, None), P("mode", "space", None, None)),
        check_vma=False,
    )
```

```python
import functools

import jax
import jax.numpy as jnp
from jax import lax
from jax.experimental import pallas as pl
from jax.experimental.pallas import tpu as pltpu
from jax.sharding import PartitionSpec as P

MESH = pl.DeviceIdType.MESH
FACES = 6


def round_up(value, multiple):
    return -(-value // multiple) * multiple


def kernel(
    groups, count, triples, coef, start, source, mean, kl,
    smoothed_out, residual_out,
    start_here, source_here, a_first, a_second, inverse_total, own_step,
    triples_here, coef_here, coefs, weights, in_first, in_second, out_first, out_second, vt, cmat,
    trade_send, trade_recv, own_sem, fetch_sem, home_sem, out_sem, plane_send, plane_recv, row_send, row_recv,
):
    local, planes, height, lanes = start.shape
    slots = local * groups
    rows = height // groups
    nfields = kl.shape[0] + 1
    padded = vt.shape[3]
    entries = weights.shape[0] // (planes * height)
    stride = planes * rows
    me = lax.axis_index("mode")
    at = lax.axis_index("space")
    has_left = at > 0
    has_right = at < count - 1

    barrier = pltpu.get_barrier_semaphore()
    for d in range(1, groups):
        pl.semaphore_signal(
            barrier, inc=1, device_id={"mode": lax.rem(me + d, groups)}, device_id_type=MESH
        )

    @pl.when(has_left)
    def _():
        pl.semaphore_signal(barrier, inc=1, device_id={"space": at - 1}, device_id_type=MESH)

    @pl.when(has_right)
    def _():
        pl.semaphore_signal(barrier, inc=1, device_id={"space": at + 1}, device_id_type=MESH)

    fields_here = [
        pltpu.make_async_copy(start, start_here, home_sem.at[0]),
        pltpu.make_async_copy(source, source_here, home_sem.at[1]),
    ]
    fetches = [
        pltpu.make_async_copy(triples, triples_here, fetch_sem.at[0]),
        pltpu.make_async_copy(coef, coef_here, fetch_sem.at[1]),
        pltpu.make_async_copy(mean, coefs.at[pl.ds(1, planes), 0], fetch_sem.at[2]),
    ] + [
        pltpu.make_async_copy(
            kl.at[:, z], coefs.at[z + 1, pl.ds(1, nfields - 1)], fetch_sem.at[3 + z]
        )
        for z in range(planes)
    ]
    for copy in fetches:
        copy.start()

    @pl.when(jnp.logical_not(has_left))
    def _():
        coefs[0] = jnp.zeros(coefs.shape[1:], jnp.float32)
        for k in range(2):
            vt[k, 0] = jnp.zeros(vt.shape[2:], jnp.float32)

    @pl.when(jnp.logical_not(has_right))
    def _():
        coefs[planes + 1] = jnp.zeros(coefs.shape[1:], jnp.float32)
        for k in range(2):
            vt[k, planes + 1] = jnp.zeros(vt.shape[2:], jnp.float32)

    @pl.when(me == 0)
    def _():
        for k in range(2):
            for z in range(planes):
                vt[k, z + 1, 0] = jnp.zeros(vt.shape[3:], jnp.float32)

    @pl.when(me == groups - 1)
    def _():
        for k in range(2):
            for z in range(planes):
                vt[k, z + 1, rows + 1] = jnp.zeros(vt.shape[3:], jnp.float32)

    far = lax.rem(at, 2)
    near = 1 - far

    def plane_of(side, i):
        return side * (planes - 1) + (1 - 2 * side) * i

    def band(ref, which):
        return ref.at[:, :, pl.ds(pl.multiple_of(which * rows, rows), rows), :]

    def modes(ref, which):
        size = local * stride
        return ref.at[pl.ds(pl.multiple_of(which * size, size), size), :].reshape(
            local, planes, rows, lanes
        )

    def ends(phase, i, target, owner):
        if phase < 2:
            z = plane_of(far, i)
            return (
                band((start, source)[phase], target).at[:, z],
                modes((in_first, in_second)[phase], owner).at[:, z],
            )
        z = plane_of(near, i)
        return (
            modes((out_first, out_second)[phase - 2], target).at[:, z],
            band((a_first, a_second)[phase - 2], owner).at[:, z],
        )

    def remote(phase, i, d):
        peer = lax.rem(me + d, groups)
        src, dst = ends(phase, i, peer, me)
        part = phase * planes + i
        return pltpu.make_async_remote_copy(
            src_ref=src, dst_ref=dst,
            send_sem=trade_send.at[part, d - 1], recv_sem=trade_recv.at[part, d - 1],
            device_id={"mode": peer}, device_id_type=MESH,
        )

    def own(phase, i):
        src, dst = ends(phase, i, me, me)
        return pltpu.make_async_copy(src, dst, own_sem.at[phase * planes + i])

    def trade_start(phase, i, after=None):
        for d in range(1, groups):
            if after is not None:
                remote(*after, d).wait_send()
            remote(phase, i, d).start()
        own(phase, i).start()

    def trade_wait_send(phase, i):
        for d in range(1, groups):
            remote(phase, i, d).wait_send()

    def trade_wait_recv(phase, i):
        for d in range(1, groups):
            remote(phase, i, d).wait_recv()
        own(phase, i).wait()

    def plane_copy(k, side):
        src, dst = 1 + side * (planes - 1), (planes + 1) * (1 - side)
        inner = (lambda z: coefs.at[z]) if k == 2 else (lambda z: vt.at[k, z, pl.ds(1, rows)])
        return pltpu.make_async_remote_copy(
            src_ref=inner(src), dst_ref=inner(dst),
            send_sem=plane_send.at[k, side], recv_sem=plane_recv.at[k, side],
            device_id={"space": at - 1 + 2 * side}, device_id_type=MESH,
        )

    def has(side):
        other = at - 1 + 2 * side
        return jnp.logical_and(other >= 0, other < count)

    def plane_start(k, side):
        @pl.when(has(side))
        def _():
            plane_copy(k, side).start()

    def plane_wait_send(k):
        for side in range(2):
            @pl.when(has(side))
            def _():
                plane_copy(k, side).wait_send()

    def plane_wait_recv(k, side):
        @pl.when(has(side))
        def _():
            plane_copy(k, 1 - side).wait_recv()

    has_up = me > 0
    has_down = me < groups - 1

    def row_copy(k, z, side):
        src, dst = (1, rows + 1) if side == 0 else (rows, 0)
        return pltpu.make_async_remote_copy(
            src_ref=vt.at[k, z + 1, src], dst_ref=vt.at[k, z + 1, dst],
            send_sem=row_send.at[k, z, side], recv_sem=row_recv.at[k, z, side],
            device_id={"mode": me - 1 if side == 0 else me + 1}, device_id_type=MESH,
        )

    def row_start(k, z):
        for side, sends in ((0, has_up), (1, has_down)):
            @pl.when(sends)
            def _():
                row_copy(k, z, side).start()

    def row_wait_send(k, z):
        for side, sends in ((0, has_up), (1, has_down)):
            @pl.when(sends)
            def _():
                row_copy(k, z, side).wait_send()

    def row_wait_recv(k, z):
        for side, gets in ((0, has_down), (1, has_up)):
            @pl.when(gets)
            def _():
                row_copy(k, z, side).wait_recv()

    pl.semaphore_wait(
        barrier, groups - 1 + has_left.astype(jnp.int32) + has_right.astype(jnp.int32)
    )
    trade_start(0, 0)
    for copy in fetches:
        copy.wait()
    for copy in fields_here:
        copy.start()
    plane_start(2, 0)
    plane_start(2, 1)

    nnz = coef_here.shape[1]
    width = cmat.shape[1]
    fields_row, rows_row, cols_row = (triples_here[i:i + 1, :] for i in range(3))
    coef_row = coef_here[...]
    row_hot = lax.broadcasted_iota(jnp.int32, (padded, nnz), 0) == rows_row
    key_hot = lax.broadcasted_iota(jnp.int32, (width, nnz), 0) == fields_row * padded + cols_row
    coef_high = coef_row.astype(jnp.bfloat16).astype(jnp.float32)
    row_one = jnp.where(row_hot, 1.0, 0.0).astype(jnp.bfloat16)
    for piece, value in enumerate((coef_high, coef_row - coef_high)):
        spread = jnp.where(key_hot, value, 0.0).astype(jnp.bfloat16)
        part = lax.dot_general(
            row_one, spread, (((1,), (1,)), ((), ())), preferred_element_type=jnp.float32
        )
        cmat[piece * padded:(piece + 1) * padded, :] = part.astype(jnp.bfloat16)
    diag = jnp.sum(
        jnp.where(jnp.logical_and(row_hot, fields_row == 0), coef_row, 0.0), axis=1, keepdims=True
    )
    real = lax.broadcasted_iota(jnp.int32, (padded, 1), 0) < slots
    diag = jnp.where(real, diag, 1.0)
    own_ids = lax.broadcasted_iota(jnp.int32, (own_step.shape[0], nnz), 0)
    own_diag = jnp.sum(
        jnp.where(jnp.logical_and(own_ids + me * local == rows_row, fields_row == 0), coef_row, 0.0),
        axis=1, keepdims=True,
    )
    own_diag = jnp.where(own_ids[:, :1] < local, own_diag, 1.0)
    own_step[...] = jnp.broadcast_to(0.8 / own_diag, own_step.shape)
    step = 0.8 / diag

    fill = jnp.zeros((padded - slots, lanes), jnp.float32)

    def fetch(ref, z, y):
        return ref[pl.ds(z * rows + y, slots, stride=stride), :]

    def spread_weights(z, y):
        base = pl.multiple_of((z * height + me * rows + y) * entries, 8)
        return weights[pl.ds(base, entries), :]

    def fill_plane(k, i, one_row):
        z = plane_of(far, i)
        one_row(z, 0)
        one_row(z, rows - 1)
        row_start(k, z)

        def inner(y, carry):
            one_row(z, y)
            return carry
        lax.fori_loop(1, rows - 1, inner, 0)
        if i == 0:
            plane_start(k, far)
        if i == planes - 1:
            plane_start(k, near)

    def relay(z, y):
        vt[0, z + 1, y + 1] = jnp.concatenate([fetch(in_first, z, y), fill], axis=0)

    for i in range(1, planes):
        trade_start(0, i)

    plane_wait_recv(2, 0)
    plane_wait_recv(2, 1)
    lane = lax.broadcasted_iota(jnp.int32, (height, lanes), 1)
    row = lax.broadcasted_iota(jnp.int32, (height, lanes), 0)
    for z in range(planes):
        for m in range(nfields):
            c = coefs[z + 1, m]
            faces = []
            for axis, size, ids in ((1, lanes, lane), (0, height, row)):
                for shift, edge in ((size - 1, size - 1), (1, 0)):
                    other = jnp.where(ids == edge, 0.0, pltpu.roll(c, shift, axis))
                    faces.append(0.5 * (c + other))
            faces.append(0.5 * (c + coefs[z + 2, m]))
            faces.append(0.5 * (c + coefs[z, m]))
            total = functools.reduce(lambda a, b: a + b, faces)
            faces[0] = jnp.where(lane == lanes - 1, 0.0, faces[0])
            faces[1] = jnp.where(lane == 0, 0.0, faces[1])
            first = z * height * entries
            for f, value in enumerate(faces + [total]):
                weights[pl.ds(first + f * nfields + m, height, stride=entries), :] = value
            if m == 0:
                inverse_total[z] = 1.0 / total
                weights[pl.ds(first + (FACES + 1) * nfields, height, stride=entries), :] = (
                    inverse_total[z]
                )

    last = planes - 1
    for i in range(planes):
        trade_wait_recv(0, i)
        fill_plane(0, i, relay)
        trade_start(1, i, after=(0, i))

    def applied(k, z, y):
        w = spread_weights(z, y)
        centre = vt[k, z + 1, y + 1]
        others = (
            pltpu.roll(centre, lanes - 1, 1), pltpu.roll(centre, 1, 1),
            vt[k, z + 1, y + 2], vt[k, z + 1, y],
            vt[k, z + 2, y + 1], vt[k, z, y + 1],
        )
        parts = []
        for m in range(nfields):
            at_total = FACES * nfields + m
            value = w[at_total:at_total + 1] * centre
            for f in range(FACES):
                at_face = f * nfields + m
                value = value - w[at_face:at_face + 1] * others[f]
            parts.append(value)
        if width > nfields * padded:
            parts.append(jnp.zeros((width - nfields * padded, lanes), jnp.float32))
        return jnp.concatenate(parts, axis=0)

    def product(k, z, y):
        x = jnp.concatenate([applied(k, z, y), applied(k, z, y + 1)], axis=1)
        high = x.astype(jnp.bfloat16)
        low = (x - high.astype(jnp.float32)).astype(jnp.bfloat16)
        both = jnp.dot(cmat[...], high, preferred_element_type=jnp.float32)
        rest = jnp.dot(cmat[:padded, :], low, preferred_element_type=jnp.float32)
        return both[:padded] + (both[padded:] + rest)

    def sweep(k, i, out, first_group, groups_here, step_here):
        z = plane_of(near, i)

        def group(t, carry):
            y = 4 * (first_group + step_here * t)
            values = [product(k, z, y), product(k, z, y + 2)]
            for j in range(4):
                out[pl.ds(z * rows + y + j, slots, stride=stride), :] = values[j // 2][
                    :slots, (j % 2) * lanes:(j % 2 + 1) * lanes
                ]
            return carry
        lax.fori_loop(0, groups_here, group, 0)

    def sweep_all(k, out, done):
        quads = rows // 4
        for i in range(planes):
            if i == 0:
                plane_wait_recv(k, near)
            if i == last:
                plane_wait_recv(k, far)
            sweep(k, i, out, 1, quads - 2, 1)
        for i in range(planes):
            row_wait_recv(k, plane_of(near, i))
            sweep(k, i, out, 0, 2, quads - 1)
            done(i)

    sweep_all(0, out_first, lambda i: None)

    def update(z, y):
        inverse = spread_weights(z, y)[(FACES + 1) * nfields:(FACES + 1) * nfields + 1]
        first = fetch(in_second, z, y) - fetch(out_first, z, y)
        first = jnp.concatenate([first, fill], axis=0)
        vt[1, z + 1, y + 1] = vt[0, z + 1, y + 1] + first * (step * inverse)

    for i in range(planes):
        trade_wait_recv(1, i)
        fill_plane(1, i, update)
        trade_start(2, i, after=(1, i))
    sweep_all(1, out_second, lambda i: trade_start(3, i))

    for copy in fields_here:
        copy.wait()
    for i in range(planes):
        trade_wait_recv(2, i)

    def make_middle(j, carry):
        gain = own_step[pl.ds(j, 1), :]
        for z in range(planes):
            first = source_here[j, z] - a_first[j, z]
            start_here[j, z] = start_here[j, z] + first * (gain * inverse_total[z])
        return carry
    lax.fori_loop(0, local, make_middle, 0)

    def results(i):
        z = plane_of(near, i)
        return [
            pltpu.make_async_copy(held.at[:, z], out.at[:, z], out_sem.at[i, n])
            for n, (held, out) in enumerate(((start_here, smoothed_out), (a_second, residual_out)))
        ]

    for i in range(planes):
        z = plane_of(near, i)
        trade_wait_recv(3, i)

        def make_outputs(j, carry):
            residual = source_here[j, z] - a_second[j, z]
            a_second[j, z] = residual
            gain = own_step[pl.ds(j, 1), :] * inverse_total[z]
            start_here[j, z] = start_here[j, z] + residual * gain
            return carry
        lax.fori_loop(0, local, make_outputs, 0)
        for copy in results(i):
            copy.start()
    for k in range(3):
        plane_wait_send(k)
        if k < 2:
            for z in range(planes):
                row_wait_send(k, z)
    for phase in (2, 3):
        for i in range(planes):
            trade_wait_send(phase, i)
    for i in range(planes):
        for copy in results(i):
            copy.wait()


def body(count, start_field, source, mean_field, kl_fields, triples, coef):
    local, planes, height, lanes = start_field.shape
    groups = lax.axis_size("mode")
    slots = local * groups
    nfields = kl_fields.shape[0] + 1
    rows = height // groups
    padded = round_up(slots, 8)
    width = round_up(nfields * padded, 16)
    entries = round_up((FACES + 1) * nfields + 1, 8)
    nnz = triples.shape[0]
    f32 = jnp.float32
    whole = jax.ShapeDtypeStruct(start_field.shape, f32)
    anywhere = pl.BlockSpec(memory_space=pl.ANY)
    dma = pltpu.SemaphoreType.DMA
    smoothed, residual = pl.pallas_call(
        functools.partial(kernel, groups, count),
        out_shape=(whole, whole),
        in_specs=[pl.BlockSpec(memory_space=pltpu.HBM)] * 6,
        out_specs=(anywhere, anywhere),
        scratch_shapes=[
            *[pltpu.VMEM(start_field.shape, f32)] * 4,
            pltpu.VMEM((planes, height, lanes), f32),
            pltpu.VMEM((round_up(local, 8), lanes), f32),
            pltpu.VMEM((3, nnz), jnp.int32),
            pltpu.VMEM((1, nnz), f32),
            pltpu.VMEM((planes + 2, nfields, height, lanes), f32),
            pltpu.VMEM((planes * height * entries, lanes), f32),
            pltpu.VMEM((slots * planes * rows, lanes), f32),
            pltpu.VMEM((slots * planes * rows, lanes), f32),
            pltpu.VMEM((slots * planes * rows, lanes), f32),
            pltpu.VMEM((slots * planes * rows, lanes), f32),
            pltpu.VMEM((2, planes + 2, rows + 2, padded, lanes), f32),
            pltpu.VMEM((2 * padded, width), jnp.bfloat16),
            dma((4 * planes, groups - 1)), dma((4 * planes, groups - 1)), dma((4 * planes,)),
            dma((3 + planes,)), dma((2,)), dma((planes, 2)),
            dma((3, 2)), dma((3, 2)), dma((2, planes, 2)), dma((2, planes, 2)),
        ],
        compiler_params=pltpu.CompilerParams(
            collective_id=0, has_side_effects=True, vmem_limit_bytes=62 * 1024 * 1024
        ),
        name="sweeps",
    )(triples.T, coef[None], start_field, source, mean_field, kl_fields)
    return smoothed, residual


def solution(mesh):
    return jax.shard_map(
        functools.partial(body, mesh.shape["space"]),
        mesh=mesh,
        in_specs=(
            P("mode", "space", None, None),
            P("mode", "space", None, None),
            P("space", None, None),
            P(None, "space", None, None),
            P(),
            P(),
        ),
        out_specs=(P("mode", "space", None, None), P("mode", "space", None, None)),
        check_vma=False,
    )
```

```python
import functools

import jax
import jax.numpy as jnp
from jax import lax
from jax.experimental import pallas as pl
from jax.experimental.pallas import tpu as pltpu
from jax.sharding import PartitionSpec as P

MESH = pl.DeviceIdType.MESH
FACES = 6


def round_up(value, multiple):
    return -(-value // multiple) * multiple


def kernel(
    groups, count, triples, coef, start, source, mean, kl,
    smoothed_out, residual_out,
    start_here, source_here, a_first, a_second, inverse_total, own_step,
    triples_here, coef_here, coefs, weights, in_first, in_second, out_first, out_second, vt, cmat,
    trade_send, trade_recv, own_sem, fetch_sem, home_sem, out_sem, plane_send, plane_recv, row_send, row_recv,
):
    local, planes, height, lanes = start.shape
    slots = local * groups
    rows = height // groups
    nfields = kl.shape[0] + 1
    padded = vt.shape[3]
    entries = weights.shape[0] // (planes * height)
    stride = planes * rows
    me = lax.axis_index("mode")
    at = lax.axis_index("space")
    has_left = at > 0
    has_right = at < count - 1

    barrier = pltpu.get_barrier_semaphore()
    for d in range(1, groups):
        pl.semaphore_signal(
            barrier, inc=1, device_id={"mode": lax.rem(me + d, groups)}, device_id_type=MESH
        )

    @pl.when(has_left)
    def _():
        pl.semaphore_signal(barrier, inc=1, device_id={"space": at - 1}, device_id_type=MESH)

    @pl.when(has_right)
    def _():
        pl.semaphore_signal(barrier, inc=1, device_id={"space": at + 1}, device_id_type=MESH)

    fields_here = [
        pltpu.make_async_copy(start, start_here, home_sem.at[0]),
        pltpu.make_async_copy(source, source_here, home_sem.at[1]),
    ]
    fetches = [
        pltpu.make_async_copy(triples, triples_here, fetch_sem.at[0]),
        pltpu.make_async_copy(coef, coef_here, fetch_sem.at[1]),
        pltpu.make_async_copy(mean, coefs.at[pl.ds(1, planes), 0], fetch_sem.at[2]),
    ] + [
        pltpu.make_async_copy(
            kl.at[:, z], coefs.at[z + 1, pl.ds(1, nfields - 1)], fetch_sem.at[3 + z]
        )
        for z in range(planes)
    ]
    for copy in fetches:
        copy.start()

    @pl.when(jnp.logical_not(has_left))
    def _():
        coefs[0] = jnp.zeros(coefs.shape[1:], jnp.float32)
        for k in range(2):
            vt[k, 0] = jnp.zeros(vt.shape[2:], jnp.float32)

    @pl.when(jnp.logical_not(has_right))
    def _():
        coefs[planes + 1] = jnp.zeros(coefs.shape[1:], jnp.float32)
        for k in range(2):
            vt[k, planes + 1] = jnp.zeros(vt.shape[2:], jnp.float32)

    @pl.when(me == 0)
    def _():
        for k in range(2):
            for z in range(planes):
                vt[k, z + 1, 0] = jnp.zeros(vt.shape[3:], jnp.float32)

    @pl.when(me == groups - 1)
    def _():
        for k in range(2):
            for z in range(planes):
                vt[k, z + 1, rows + 1] = jnp.zeros(vt.shape[3:], jnp.float32)

    far = lax.rem(at, 2)
    near = 1 - far

    def plane_of(side, i):
        return side * (planes - 1) + (1 - 2 * side) * i

    def band(ref, which):
        return ref.at[:, :, pl.ds(pl.multiple_of(which * rows, rows), rows), :]

    def modes(ref, which):
        size = local * stride
        return ref.at[pl.ds(pl.multiple_of(which * size, size), size), :].reshape(
            local, planes, rows, lanes
        )

    def ends(phase, i, target, owner):
        if phase < 2:
            z = plane_of(far, i)
            return (
                band((start, source)[phase], target).at[:, z],
                modes((in_first, in_second)[phase], owner).at[:, z],
            )
        z = plane_of(near, i)
        return (
            modes((out_first, out_second)[phase - 2], target).at[:, z],
            band((a_first, a_second)[phase - 2], owner).at[:, z],
        )

    def remote(phase, i, d):
        peer = lax.rem(me + d, groups)
        src, dst = ends(phase, i, peer, me)
        part = phase * planes + i
        return pltpu.make_async_remote_copy(
            src_ref=src, dst_ref=dst,
            send_sem=trade_send.at[part, d - 1], recv_sem=trade_recv.at[part, d - 1],
            device_id={"mode": peer}, device_id_type=MESH,
        )

    def own(phase, i):
        src, dst = ends(phase, i, me, me)
        return pltpu.make_async_copy(src, dst, own_sem.at[phase * planes + i])

    def trade_start(phase, i, after=None):
        for d in range(1, groups):
            if after is not None:
                remote(*after, d).wait_send()
            remote(phase, i, d).start()
        own(phase, i).start()

    def trade_wait_send(phase, i):
        for d in range(1, groups):
            remote(phase, i, d).wait_send()

    def trade_wait_recv(phase, i):
        for d in range(1, groups):
            remote(phase, i, d).wait_recv()
        own(phase, i).wait()

    def plane_copy(k, side):
        src, dst = 1 + side * (planes - 1), (planes + 1) * (1 - side)
        inner = (lambda z: coefs.at[z]) if k == 2 else (lambda z: vt.at[k, z, pl.ds(1, rows)])
        return pltpu.make_async_remote_copy(
            src_ref=inner(src), dst_ref=inner(dst),
            send_sem=plane_send.at[k, side], recv_sem=plane_recv.at[k, side],
            device_id={"space": at - 1 + 2 * side}, device_id_type=MESH,
        )

    def has(side):
        other = at - 1 + 2 * side
        return jnp.logical_and(other >= 0, other < count)

    def plane_start(k, side):
        @pl.when(has(side))
        def _():
            plane_copy(k, side).start()

    def plane_wait_send(k):
        for side in range(2):
            @pl.when(has(side))
            def _():
                plane_copy(k, side).wait_send()

    def plane_wait_recv(k, side):
        @pl.when(has(side))
        def _():
            plane_copy(k, 1 - side).wait_recv()

    has_up = me > 0
    has_down = me < groups - 1

    def row_copy(k, z, side):
        src, dst = (1, rows + 1) if side == 0 else (rows, 0)
        return pltpu.make_async_remote_copy(
            src_ref=vt.at[k, z + 1, src], dst_ref=vt.at[k, z + 1, dst],
            send_sem=row_send.at[k, z, side], recv_sem=row_recv.at[k, z, side],
            device_id={"mode": me - 1 if side == 0 else me + 1}, device_id_type=MESH,
        )

    def row_start(k, z):
        for side, sends in ((0, has_up), (1, has_down)):
            @pl.when(sends)
            def _():
                row_copy(k, z, side).start()

    def row_wait_send(k, z):
        for side, sends in ((0, has_up), (1, has_down)):
            @pl.when(sends)
            def _():
                row_copy(k, z, side).wait_send()

    def row_wait_recv(k, z):
        for side, gets in ((0, has_down), (1, has_up)):
            @pl.when(gets)
            def _():
                row_copy(k, z, side).wait_recv()

    pl.semaphore_wait(
        barrier, groups - 1 + has_left.astype(jnp.int32) + has_right.astype(jnp.int32)
    )
    trade_start(0, 0)
    for copy in fetches:
        copy.wait()
    for copy in fields_here:
        copy.start()
    plane_start(2, 0)
    plane_start(2, 1)

    nnz = coef_here.shape[1]
    width = cmat.shape[1]
    fields_row, rows_row, cols_row = (triples_here[i:i + 1, :] for i in range(3))
    coef_row = coef_here[...]
    row_hot = lax.broadcasted_iota(jnp.int32, (padded, nnz), 0) == rows_row
    key_hot = lax.broadcasted_iota(jnp.int32, (width, nnz), 0) == fields_row * padded + cols_row
    coef_high = coef_row.astype(jnp.bfloat16).astype(jnp.float32)
    row_one = jnp.where(row_hot, 1.0, 0.0).astype(jnp.bfloat16)
    for piece, value in enumerate((coef_high, coef_row - coef_high)):
        spread = jnp.where(key_hot, value, 0.0).astype(jnp.bfloat16)
        part = lax.dot_general(
            row_one, spread, (((1,), (1,)), ((), ())), preferred_element_type=jnp.float32
        )
        cmat[piece * padded:(piece + 1) * padded, :] = part.astype(jnp.bfloat16)
    diag = jnp.sum(
        jnp.where(jnp.logical_and(row_hot, fields_row == 0), coef_row, 0.0), axis=1, keepdims=True
    )
    real = lax.broadcasted_iota(jnp.int32, (padded, 1), 0) < slots
    diag = jnp.where(real, diag, 1.0)
    own_ids = lax.broadcasted_iota(jnp.int32, (own_step.shape[0], nnz), 0)
    own_diag = jnp.sum(
        jnp.where(jnp.logical_and(own_ids + me * local == rows_row, fields_row == 0), coef_row, 0.0),
        axis=1, keepdims=True,
    )
    own_diag = jnp.where(own_ids[:, :1] < local, own_diag, 1.0)
    own_step[...] = jnp.broadcast_to(0.8 / own_diag, own_step.shape)
    step = 0.8 / diag

    fill = jnp.zeros((padded - slots, lanes), jnp.float32)

    def fetch(ref, z, y):
        return ref[pl.ds(z * rows + y, slots, stride=stride), :]

    def spread_weights(z, y):
        base = pl.multiple_of((z * height + me * rows + y) * entries, 8)
        return weights[pl.ds(base, entries), :]

    def fill_plane(k, i, one_row):
        z = plane_of(far, i)
        one_row(z, 0)
        one_row(z, rows - 1)
        row_start(k, z)

        def inner(y, carry):
            one_row(z, y)
            return carry
        lax.fori_loop(1, rows - 1, inner, 0)
        if i == 0:
            plane_start(k, far)
        if i == planes - 1:
            plane_start(k, near)

    def relay(z, y):
        vt[0, z + 1, y + 1] = jnp.concatenate([fetch(in_first, z, y), fill], axis=0)

    for i in range(1, planes):
        trade_start(0, i)

    plane_wait_recv(2, 0)
    plane_wait_recv(2, 1)
    lane = lax.broadcasted_iota(jnp.int32, (height, lanes), 1)
    row = lax.broadcasted_iota(jnp.int32, (height, lanes), 0)
    for z in range(planes):
        for m in range(nfields):
            c = coefs[z + 1, m]
            faces = []
            for axis, size, ids in ((1, lanes, lane), (0, height, row)):
                for shift, edge in ((size - 1, size - 1), (1, 0)):
                    other = jnp.where(ids == edge, 0.0, pltpu.roll(c, shift, axis))
                    faces.append(0.5 * (c + other))
            faces.append(0.5 * (c + coefs[z + 2, m]))
            faces.append(0.5 * (c + coefs[z, m]))
            total = functools.reduce(lambda a, b: a + b, faces)
            faces[0] = jnp.where(lane == lanes - 1, 0.0, faces[0])
            faces[1] = jnp.where(lane == 0, 0.0, faces[1])
            first = z * height * entries
            for f, value in enumerate(faces + [total]):
                weights[pl.ds(first + f * nfields + m, height, stride=entries), :] = value
            if m == 0:
                inverse_total[z] = 1.0 / total
                weights[pl.ds(first + (FACES + 1) * nfields, height, stride=entries), :] = (
                    inverse_total[z]
                )

    last = planes - 1
    for i in range(planes):
        trade_start(1, i, after=(0, i))
        trade_wait_recv(0, i)
        fill_plane(0, i, relay)

    def applied(k, z, y):
        w = spread_weights(z, y)
        centre = vt[k, z + 1, y + 1]
        others = (
            pltpu.roll(centre, lanes - 1, 1), pltpu.roll(centre, 1, 1),
            vt[k, z + 1, y + 2], vt[k, z + 1, y],
            vt[k, z + 2, y + 1], vt[k, z, y + 1],
        )
        parts = []
        for m in range(nfields):
            at_total = FACES * nfields + m
            value = w[at_total:at_total + 1] * centre
            for f in range(FACES):
                at_face = f * nfields + m
                value = value - w[at_face:at_face + 1] * others[f]
            parts.append(value)
        if width > nfields * padded:
            parts.append(jnp.zeros((width - nfields * padded, lanes), jnp.float32))
        return jnp.concatenate(parts, axis=0)

    def product(k, z, y):
        x = jnp.concatenate([applied(k, z, y), applied(k, z, y + 1)], axis=1)
        high = x.astype(jnp.bfloat16)
        low = (x - high.astype(jnp.float32)).astype(jnp.bfloat16)
        both = jnp.dot(cmat[...], high, preferred_element_type=jnp.float32)
        rest = jnp.dot(cmat[:padded, :], low, preferred_element_type=jnp.float32)
        return both[:padded] + (both[padded:] + rest)

    def sweep(k, i, out, first_group, groups_here, step_here):
        z = plane_of(near, i)

        def group(t, carry):
            y = 4 * (first_group + step_here * t)
            values = [product(k, z, y), product(k, z, y + 2)]
            for j in range(4):
                out[pl.ds(z * rows + y + j, slots, stride=stride), :] = values[j // 2][
                    :slots, (j % 2) * lanes:(j % 2 + 1) * lanes
                ]
            return carry
        lax.fori_loop(0, groups_here, group, 0)

    def sweep_all(k, out, done):
        quads = rows // 4
        for i in range(planes):
            if i == 0:
                plane_wait_recv(k, near)
            if i == last:
                plane_wait_recv(k, far)
            sweep(k, i, out, 1, quads - 2, 1)
        for i in range(planes):
            row_wait_recv(k, plane_of(near, i))
            sweep(k, i, out, 0, 2, quads - 1)
            done(i)

    sweep_all(0, out_first, lambda i: None)

    def update(z, y):
        inverse = spread_weights(z, y)[(FACES + 1) * nfields:(FACES + 1) * nfields + 1]
        first = fetch(in_second, z, y) - fetch(out_first, z, y)
        first = jnp.concatenate([first, fill], axis=0)
        vt[1, z + 1, y + 1] = vt[0, z + 1, y + 1] + first * (step * inverse)

    for i in range(planes):
        if i == 0:
            trade_start(2, i, after=(1, i))
        trade_wait_recv(1, i)
        fill_plane(1, i, update)
        if i > 0:
            trade_start(2, i, after=(1, i))
    sweep_all(1, out_second, lambda i: trade_start(3, i))

    for copy in fields_here:
        copy.wait()
    for i in range(planes):
        trade_wait_recv(2, i)

    def make_middle(j, carry):
        gain = own_step[pl.ds(j, 1), :]
        for z in range(planes):
            first = source_here[j, z] - a_first[j, z]
            start_here[j, z] = start_here[j, z] + first * (gain * inverse_total[z])
        return carry
    lax.fori_loop(0, local, make_middle, 0)

    def results(i):
        z = plane_of(near, i)
        return [
            pltpu.make_async_copy(held.at[:, z], out.at[:, z], out_sem.at[i, n])
            for n, (held, out) in enumerate(((start_here, smoothed_out), (a_second, residual_out)))
        ]

    for i in range(planes):
        z = plane_of(near, i)
        trade_wait_recv(3, i)

        def make_outputs(j, carry):
            residual = source_here[j, z] - a_second[j, z]
            a_second[j, z] = residual
            gain = own_step[pl.ds(j, 1), :] * inverse_total[z]
            start_here[j, z] = start_here[j, z] + residual * gain
            return carry
        lax.fori_loop(0, local, make_outputs, 0)
        for copy in results(i):
            copy.start()
    for k in range(3):
        plane_wait_send(k)
        if k < 2:
            for z in range(planes):
                row_wait_send(k, z)
    for phase in (2, 3):
        for i in range(planes):
            trade_wait_send(phase, i)
    for i in range(planes):
        for copy in results(i):
            copy.wait()


def place(smoothed, residual, smoothed_out, residual_out, sem):
    copies = [
        pltpu.make_async_copy(ref.at[j], out.at[j], sem.at[n, j])
        for n, (ref, out) in enumerate(((smoothed, smoothed_out), (residual, residual_out)))
        for j in range(ref.shape[0])
    ]
    for copy in copies:
        copy.start()
    for copy in copies:
        copy.wait()


def body(count, start_field, source, mean_field, kl_fields, triples, coef):
    local, planes, height, lanes = start_field.shape
    groups = lax.axis_size("mode")
    slots = local * groups
    nfields = kl_fields.shape[0] + 1
    rows = height // groups
    padded = round_up(slots, 8)
    width = round_up(nfields * padded, 16)
    entries = round_up((FACES + 1) * nfields + 1, 8)
    nnz = triples.shape[0]
    f32 = jnp.float32
    whole = jax.ShapeDtypeStruct(start_field.shape, f32)
    anywhere = pl.BlockSpec(memory_space=pl.ANY)
    dma = pltpu.SemaphoreType.DMA
    smoothed, residual = pl.pallas_call(
        functools.partial(kernel, groups, count),
        out_shape=(whole, whole),
        in_specs=[pl.BlockSpec(memory_space=pltpu.HBM)] * 6,
        out_specs=(anywhere, anywhere),
        scratch_shapes=[
            *[pltpu.VMEM(start_field.shape, f32)] * 4,
            pltpu.VMEM((planes, height, lanes), f32),
            pltpu.VMEM((round_up(local, 8), lanes), f32),
            pltpu.VMEM((3, nnz), jnp.int32),
            pltpu.VMEM((1, nnz), f32),
            pltpu.VMEM((planes + 2, nfields, height, lanes), f32),
            pltpu.VMEM((planes * height * entries, lanes), f32),
            pltpu.VMEM((slots * planes * rows, lanes), f32),
            pltpu.VMEM((slots * planes * rows, lanes), f32),
            pltpu.VMEM((slots * planes * rows, lanes), f32),
            pltpu.VMEM((slots * planes * rows, lanes), f32),
            pltpu.VMEM((2, planes + 2, rows + 2, padded, lanes), f32),
            pltpu.VMEM((2 * padded, width), jnp.bfloat16),
            dma((4 * planes, groups - 1)), dma((4 * planes, groups - 1)), dma((4 * planes,)),
            dma((3 + planes,)), dma((2,)), dma((planes, 2)),
            dma((3, 2)), dma((3, 2)), dma((2, planes, 2)), dma((2, planes, 2)),
        ],
        compiler_params=pltpu.CompilerParams(
            collective_id=0, has_side_effects=True, vmem_limit_bytes=62 * 1024 * 1024
        ),
        name="sweeps",
    )(triples.T, coef[None], start_field, source, mean_field, kl_fields)
    return pl.pallas_call(
        place,
        out_shape=(whole, whole),
        in_specs=[anywhere, anywhere],
        out_specs=(anywhere, anywhere),
        scratch_shapes=[dma((2, local))],
        compiler_params=pltpu.CompilerParams(vmem_limit_bytes=62 * 1024 * 1024),
        name="place",
    )(smoothed, residual)


def solution(mesh):
    return jax.shard_map(
        functools.partial(body, mesh.shape["space"]),
        mesh=mesh,
        in_specs=(
            P("mode", "space", None, None),
            P("mode", "space", None, None),
            P("space", None, None),
            P(None, "space", None, None),
            P(),
            P(),
        ),
        out_specs=(P("mode", "space", None, None), P("mode", "space", None, None)),
        check_vma=False,
    )
```

```python
import functools

import jax
import jax.numpy as jnp
from jax import lax
from jax.experimental import pallas as pl
from jax.experimental.pallas import tpu as pltpu
from jax.sharding import PartitionSpec as P

MESH = pl.DeviceIdType.MESH
FACES = 6


def round_up(value, multiple):
    return -(-value // multiple) * multiple


def kernel(
    groups, count, triples, coef, start, source, mean, kl,
    smoothed_out, residual_out,
    start_here, source_here, a_first, a_second, inverse_total, own_step,
    triples_here, coef_here, coefs, weights, in_first, in_second, out_first, out_second, vt, cmat,
    trade_send, trade_recv, own_sem, fetch_sem, home_sem, out_sem, plane_send, plane_recv, row_send, row_recv,
):
    local, planes, height, lanes = start.shape
    slots = local * groups
    rows = height // groups
    nfields = kl.shape[0] + 1
    padded = vt.shape[3]
    entries = weights.shape[0] // (planes * height)
    stride = planes * rows
    me = lax.axis_index("mode")
    at = lax.axis_index("space")
    has_left = at > 0
    has_right = at < count - 1

    barrier = pltpu.get_barrier_semaphore()
    for d in range(1, groups):
        pl.semaphore_signal(
            barrier, inc=1, device_id={"mode": lax.rem(me + d, groups)}, device_id_type=MESH
        )

    @pl.when(has_left)
    def _():
        pl.semaphore_signal(barrier, inc=1, device_id={"space": at - 1}, device_id_type=MESH)

    @pl.when(has_right)
    def _():
        pl.semaphore_signal(barrier, inc=1, device_id={"space": at + 1}, device_id_type=MESH)

    fields_here = [
        pltpu.make_async_copy(start, start_here, home_sem.at[0]),
        pltpu.make_async_copy(source, source_here, home_sem.at[1]),
    ]
    fetches = [
        pltpu.make_async_copy(triples, triples_here, fetch_sem.at[0]),
        pltpu.make_async_copy(coef, coef_here, fetch_sem.at[1]),
        pltpu.make_async_copy(mean, coefs.at[pl.ds(1, planes), 0], fetch_sem.at[2]),
    ] + [
        pltpu.make_async_copy(
            kl.at[:, z], coefs.at[z + 1, pl.ds(1, nfields - 1)], fetch_sem.at[3 + z]
        )
        for z in range(planes)
    ]
    for copy in fetches:
        copy.start()

    @pl.when(jnp.logical_not(has_left))
    def _():
        coefs[0] = jnp.zeros(coefs.shape[1:], jnp.float32)
        for k in range(2):
            vt[k, 0] = jnp.zeros(vt.shape[2:], jnp.float32)

    @pl.when(jnp.logical_not(has_right))
    def _():
        coefs[planes + 1] = jnp.zeros(coefs.shape[1:], jnp.float32)
        for k in range(2):
            vt[k, planes + 1] = jnp.zeros(vt.shape[2:], jnp.float32)

    @pl.when(me == 0)
    def _():
        for k in range(2):
            for z in range(planes):
                vt[k, z + 1, 0] = jnp.zeros(vt.shape[3:], jnp.float32)

    @pl.when(me == groups - 1)
    def _():
        for k in range(2):
            for z in range(planes):
                vt[k, z + 1, rows + 1] = jnp.zeros(vt.shape[3:], jnp.float32)

    far = lax.rem(at, 2)
    near = 1 - far

    def plane_of(side, i):
        return side * (planes - 1) + (1 - 2 * side) * i

    def band(ref, which):
        return ref.at[:, :, pl.ds(pl.multiple_of(which * rows, rows), rows), :]

    def modes(ref, which):
        size = local * stride
        return ref.at[pl.ds(pl.multiple_of(which * size, size), size), :].reshape(
            local, planes, rows, lanes
        )

    def ends(phase, i, target, owner):
        if phase < 2:
            z = plane_of(far, i)
            return (
                band((start, source)[phase], target).at[:, z],
                modes((in_first, in_second)[phase], owner).at[:, z],
            )
        z = plane_of(near, i)
        return (
            modes((out_first, out_second)[phase - 2], target).at[:, z],
            band((a_first, a_second)[phase - 2], owner).at[:, z],
        )

    def remote(phase, i, d):
        peer = lax.rem(me + d, groups)
        src, dst = ends(phase, i, peer, me)
        part = phase * planes + i
        return pltpu.make_async_remote_copy(
            src_ref=src, dst_ref=dst,
            send_sem=trade_send.at[part, d - 1], recv_sem=trade_recv.at[part, d - 1],
            device_id={"mode": peer}, device_id_type=MESH,
        )

    def own(phase, i):
        src, dst = ends(phase, i, me, me)
        return pltpu.make_async_copy(src, dst, own_sem.at[phase * planes + i])

    def trade_start(phase, i, after=None):
        for d in range(1, groups):
            if after is not None:
                remote(*after, d).wait_send()
            remote(phase, i, d).start()
        own(phase, i).start()

    def trade_wait_send(phase, i):
        for d in range(1, groups):
            remote(phase, i, d).wait_send()

    def trade_wait_recv(phase, i):
        for d in range(1, groups):
            remote(phase, i, d).wait_recv()
        own(phase, i).wait()

    def plane_copy(k, side):
        src, dst = 1 + side * (planes - 1), (planes + 1) * (1 - side)
        inner = (lambda z: coefs.at[z]) if k == 2 else (lambda z: vt.at[k, z, pl.ds(1, rows)])
        return pltpu.make_async_remote_copy(
            src_ref=inner(src), dst_ref=inner(dst),
            send_sem=plane_send.at[k, side], recv_sem=plane_recv.at[k, side],
            device_id={"space": at - 1 + 2 * side}, device_id_type=MESH,
        )

    def has(side):
        other = at - 1 + 2 * side
        return jnp.logical_and(other >= 0, other < count)

    def plane_start(k, side):
        @pl.when(has(side))
        def _():
            plane_copy(k, side).start()

    def plane_wait_send(k):
        for side in range(2):
            @pl.when(has(side))
            def _():
                plane_copy(k, side).wait_send()

    def plane_wait_recv(k, side):
        @pl.when(has(side))
        def _():
            plane_copy(k, 1 - side).wait_recv()

    has_up = me > 0
    has_down = me < groups - 1

    def row_copy(k, z, side):
        src, dst = (1, rows + 1) if side == 0 else (rows, 0)
        return pltpu.make_async_remote_copy(
            src_ref=vt.at[k, z + 1, src], dst_ref=vt.at[k, z + 1, dst],
            send_sem=row_send.at[k, z, side], recv_sem=row_recv.at[k, z, side],
            device_id={"mode": me - 1 if side == 0 else me + 1}, device_id_type=MESH,
        )

    def row_start(k, z):
        for side, sends in ((0, has_up), (1, has_down)):
            @pl.when(sends)
            def _():
                row_copy(k, z, side).start()

    def row_wait_send(k, z):
        for side, sends in ((0, has_up), (1, has_down)):
            @pl.when(sends)
            def _():
                row_copy(k, z, side).wait_send()

    def row_wait_recv(k, z):
        for side, gets in ((0, has_down), (1, has_up)):
            @pl.when(gets)
            def _():
                row_copy(k, z, side).wait_recv()

    pl.semaphore_wait(
        barrier, groups - 1 + has_left.astype(jnp.int32) + has_right.astype(jnp.int32)
    )
    trade_start(0, 0)
    for copy in fetches:
        copy.wait()
    for copy in fields_here:
        copy.start()
    plane_start(2, 0)
    plane_start(2, 1)

    nnz = coef_here.shape[1]
    width = cmat.shape[1]
    fields_row, rows_row, cols_row = (triples_here[i:i + 1, :] for i in range(3))
    coef_row = coef_here[...]
    row_hot = lax.broadcasted_iota(jnp.int32, (padded, nnz), 0) == rows_row
    key_hot = lax.broadcasted_iota(jnp.int32, (width, nnz), 0) == fields_row * padded + cols_row
    coef_high = coef_row.astype(jnp.bfloat16).astype(jnp.float32)
    row_one = jnp.where(row_hot, 1.0, 0.0).astype(jnp.bfloat16)
    for piece, value in enumerate((coef_high, coef_row - coef_high)):
        spread = jnp.where(key_hot, value, 0.0).astype(jnp.bfloat16)
        part = lax.dot_general(
            row_one, spread, (((1,), (1,)), ((), ())), preferred_element_type=jnp.float32
        )
        cmat[piece * padded:(piece + 1) * padded, :] = part.astype(jnp.bfloat16)
    diag = jnp.sum(
        jnp.where(jnp.logical_and(row_hot, fields_row == 0), coef_row, 0.0), axis=1, keepdims=True
    )
    real = lax.broadcasted_iota(jnp.int32, (padded, 1), 0) < slots
    diag = jnp.where(real, diag, 1.0)
    own_ids = lax.broadcasted_iota(jnp.int32, (own_step.shape[0], nnz), 0)
    own_diag = jnp.sum(
        jnp.where(jnp.logical_and(own_ids + me * local == rows_row, fields_row == 0), coef_row, 0.0),
        axis=1, keepdims=True,
    )
    own_diag = jnp.where(own_ids[:, :1] < local, own_diag, 1.0)
    own_step[...] = jnp.broadcast_to(0.8 / own_diag, own_step.shape)
    step = 0.8 / diag

    fill = jnp.zeros((padded - slots, lanes), jnp.float32)

    def fetch(ref, z, y):
        return ref[pl.ds(z * rows + y, slots, stride=stride), :]

    def spread_weights(z, y):
        base = pl.multiple_of((z * height + me * rows + y) * entries, 8)
        return weights[pl.ds(base, entries), :]

    def fill_plane(k, i, one_row):
        z = plane_of(far, i)
        one_row(z, 0)
        one_row(z, rows - 1)
        row_start(k, z)

        def inner(y, carry):
            one_row(z, y)
            return carry
        lax.fori_loop(1, rows - 1, inner, 0)
        if i == 0:
            plane_start(k, far)
        if i == planes - 1:
            plane_start(k, near)

    def relay(z, y):
        vt[0, z + 1, y + 1] = jnp.concatenate([fetch(in_first, z, y), fill], axis=0)

    for i in range(1, planes):
        trade_start(0, i)

    plane_wait_recv(2, 0)
    plane_wait_recv(2, 1)
    lane = lax.broadcasted_iota(jnp.int32, (height, lanes), 1)
    row = lax.broadcasted_iota(jnp.int32, (height, lanes), 0)
    for z in range(planes):
        for m in range(nfields):
            c = coefs[z + 1, m]
            faces = []
            for axis, size, ids in ((1, lanes, lane), (0, height, row)):
                for shift, edge in ((size - 1, size - 1), (1, 0)):
                    other = jnp.where(ids == edge, 0.0, pltpu.roll(c, shift, axis))
                    faces.append(0.5 * (c + other))
            faces.append(0.5 * (c + coefs[z + 2, m]))
            faces.append(0.5 * (c + coefs[z, m]))
            total = functools.reduce(lambda a, b: a + b, faces)
            faces[0] = jnp.where(lane == lanes - 1, 0.0, faces[0])
            faces[1] = jnp.where(lane == 0, 0.0, faces[1])
            first = z * height * entries
            for f, value in enumerate(faces + [total]):
                weights[pl.ds(first + f * nfields + m, height, stride=entries), :] = value
            if m == 0:
                inverse_total[z] = 1.0 / total
                weights[pl.ds(first + (FACES + 1) * nfields, height, stride=entries), :] = (
                    inverse_total[z]
                )

    last = planes - 1
    for i in range(planes):
        trade_wait_recv(0, i)
        fill_plane(0, i, relay)
        trade_start(1, i, after=(0, i))

    def applied(k, z, y):
        w = spread_weights(z, y)
        centre = vt[k, z + 1, y + 1]
        others = (
            pltpu.roll(centre, lanes - 1, 1), pltpu.roll(centre, 1, 1),
            vt[k, z + 1, y + 2], vt[k, z + 1, y],
            vt[k, z + 2, y + 1], vt[k, z, y + 1],
        )
        parts = []
        for m in range(nfields):
            at_total = FACES * nfields + m
            value = w[at_total:at_total + 1] * centre
            for f in range(FACES):
                at_face = f * nfields + m
                value = value - w[at_face:at_face + 1] * others[f]
            parts.append(value)
        if width > nfields * padded:
            parts.append(jnp.zeros((width - nfields * padded, lanes), jnp.float32))
        return jnp.concatenate(parts, axis=0)

    def product(k, z, y):
        x = jnp.concatenate([applied(k, z, y), applied(k, z, y + 1)], axis=1)
        high = x.astype(jnp.bfloat16)
        low = (x - high.astype(jnp.float32)).astype(jnp.bfloat16)
        both = jnp.dot(cmat[...], high, preferred_element_type=jnp.float32)
        rest = jnp.dot(cmat[:padded, :], low, preferred_element_type=jnp.float32)
        return both[:padded] + (both[padded:] + rest)

    def sweep(k, i, out, first_group, groups_here, step_here):
        z = plane_of(near, i)

        def group(t, carry):
            y = 4 * (first_group + step_here * t)
            values = [product(k, z, y), product(k, z, y + 2)]
            for j in range(4):
                out[pl.ds(z * rows + y + j, slots, stride=stride), :] = values[j // 2][
                    :slots, (j % 2) * lanes:(j % 2 + 1) * lanes
                ]
            return carry
        lax.fori_loop(0, groups_here, group, 0)

    def sweep_all(k, out, done):
        quads = rows // 4
        for i in range(planes):
            if i == 0:
                plane_wait_recv(k, near)
            if i == last:
                plane_wait_recv(k, far)
            sweep(k, i, out, 1, quads - 2, 1)
        for i in range(planes):
            row_wait_recv(k, plane_of(near, i))
            sweep(k, i, out, 0, 2, quads - 1)
            done(i)

    sweep_all(0, out_first, lambda i: None)

    def update(z, y):
        inverse = spread_weights(z, y)[(FACES + 1) * nfields:(FACES + 1) * nfields + 1]
        first = fetch(in_second, z, y) - fetch(out_first, z, y)
        first = jnp.concatenate([first, fill], axis=0)
        vt[1, z + 1, y + 1] = vt[0, z + 1, y + 1] + first * (step * inverse)

    for i in range(planes):
        trade_wait_recv(1, i)
        fill_plane(1, i, update)
        trade_start(2, i, after=(1, i))
    sweep_all(1, out_second, lambda i: trade_start(3, i))

    for copy in fields_here:
        copy.wait()
    for i in range(planes):
        trade_wait_recv(2, i)

    def make_middle(j, carry):
        gain = own_step[pl.ds(j, 1), :]
        for z in range(planes):
            first = source_here[j, z] - a_first[j, z]
            start_here[j, z] = start_here[j, z] + first * (gain * inverse_total[z])
        return carry
    lax.fori_loop(0, local, make_middle, 0)

    def results(i):
        z = plane_of(near, i)
        return [
            pltpu.make_async_copy(held.at[:, z], out.at[:, z], out_sem.at[i, n])
            for n, (held, out) in enumerate(((start_here, smoothed_out), (a_second, residual_out)))
        ]

    for i in range(planes):
        z = plane_of(near, i)
        trade_wait_recv(3, i)

        def make_outputs(j, carry):
            residual = source_here[j, z] - a_second[j, z]
            a_second[j, z] = residual
            gain = own_step[pl.ds(j, 1), :] * inverse_total[z]
            start_here[j, z] = start_here[j, z] + residual * gain
            return carry
        lax.fori_loop(0, local, make_outputs, 0)
        for copy in results(i):
            copy.start()
    for k in range(3):
        plane_wait_send(k)
        if k < 2:
            for z in range(planes):
                row_wait_send(k, z)
    for phase in (2, 3):
        for i in range(planes):
            trade_wait_send(phase, i)
    for i in range(planes):
        for copy in results(i):
            copy.wait()


def place(smoothed, residual, smoothed_out, residual_out, held, sem):
    triples = [
        (ref.at[j], held.at[n, j], out.at[j], sem.at[n, j])
        for j in range(smoothed.shape[0])
        for n, (ref, out) in enumerate(((smoothed, smoothed_out), (residual, residual_out)))
    ]
    inward = [pltpu.make_async_copy(ref, kept, which.at[0]) for ref, kept, _, which in triples]
    outward = [pltpu.make_async_copy(kept, out, which.at[1]) for _, kept, out, which in triples]
    for copy in inward:
        copy.start()
    for arriving, leaving in zip(inward, outward):
        arriving.wait()
        leaving.start()
    for copy in outward:
        copy.wait()


def body(count, start_field, source, mean_field, kl_fields, triples, coef):
    local, planes, height, lanes = start_field.shape
    groups = lax.axis_size("mode")
    slots = local * groups
    nfields = kl_fields.shape[0] + 1
    rows = height // groups
    padded = round_up(slots, 8)
    width = round_up(nfields * padded, 16)
    entries = round_up((FACES + 1) * nfields + 1, 8)
    nnz = triples.shape[0]
    f32 = jnp.float32
    whole = jax.ShapeDtypeStruct(start_field.shape, f32)
    anywhere = pl.BlockSpec(memory_space=pl.ANY)
    dma = pltpu.SemaphoreType.DMA
    smoothed, residual = pl.pallas_call(
        functools.partial(kernel, groups, count),
        out_shape=(whole, whole),
        in_specs=[pl.BlockSpec(memory_space=pltpu.HBM)] * 6,
        out_specs=(anywhere, anywhere),
        scratch_shapes=[
            *[pltpu.VMEM(start_field.shape, f32)] * 4,
            pltpu.VMEM((planes, height, lanes), f32),
            pltpu.VMEM((round_up(local, 8), lanes), f32),
            pltpu.VMEM((3, nnz), jnp.int32),
            pltpu.VMEM((1, nnz), f32),
            pltpu.VMEM((planes + 2, nfields, height, lanes), f32),
            pltpu.VMEM((planes * height * entries, lanes), f32),
            pltpu.VMEM((slots * planes * rows, lanes), f32),
            pltpu.VMEM((slots * planes * rows, lanes), f32),
            pltpu.VMEM((slots * planes * rows, lanes), f32),
            pltpu.VMEM((slots * planes * rows, lanes), f32),
            pltpu.VMEM((2, planes + 2, rows + 2, padded, lanes), f32),
            pltpu.VMEM((2 * padded, width), jnp.bfloat16),
            dma((4 * planes, groups - 1)), dma((4 * planes, groups - 1)), dma((4 * planes,)),
            dma((3 + planes,)), dma((2,)), dma((planes, 2)),
            dma((3, 2)), dma((3, 2)), dma((2, planes, 2)), dma((2, planes, 2)),
        ],
        compiler_params=pltpu.CompilerParams(
            collective_id=0, has_side_effects=True, vmem_limit_bytes=62 * 1024 * 1024
        ),
        name="sweeps",
    )(triples.T, coef[None], start_field, source, mean_field, kl_fields)
    return pl.pallas_call(
        place,
        out_shape=(whole, whole),
        in_specs=[anywhere, anywhere],
        out_specs=(anywhere, anywhere),
        scratch_shapes=[pltpu.VMEM((2, *start_field.shape), f32), dma((2, local, 2))],
        compiler_params=pltpu.CompilerParams(vmem_limit_bytes=62 * 1024 * 1024),
        name="place",
    )(smoothed, residual)


def solution(mesh):
    return jax.shard_map(
        functools.partial(body, mesh.shape["space"]),
        mesh=mesh,
        in_specs=(
            P("mode", "space", None, None),
            P("mode", "space", None, None),
            P("space", None, None),
            P(None, "space", None, None),
            P(),
            P(),
        ),
        out_specs=(P("mode", "space", None, None), P("mode", "space", None, None)),
        check_vma=False,
    )
```

```python
import functools

import jax
import jax.numpy as jnp
from jax import lax
from jax.experimental import pallas as pl
from jax.experimental.pallas import tpu as pltpu
from jax.sharding import PartitionSpec as P

MESH = pl.DeviceIdType.MESH
FACES = 6


def round_up(value, multiple):
    return -(-value // multiple) * multiple


def kernel(
    groups, count, triples, coef, start, source, mean, kl,
    smoothed_out, residual_out,
    start_here, source_here, a_first, a_second, inverse_total, own_step,
    triples_here, coef_here, coefs, weights, in_first, in_second, out_first, out_second, vt, cmat,
    trade_send, trade_recv, own_sem, fetch_sem, home_sem, out_sem, plane_send, plane_recv, row_send, row_recv,
):
    local, planes, height, lanes = start.shape
    slots = local * groups
    rows = height // groups
    nfields = kl.shape[0] + 1
    padded = vt.shape[3]
    entries = weights.shape[0] // (planes * height)
    stride = planes * rows
    me = lax.axis_index("mode")
    at = lax.axis_index("space")
    has_left = at > 0
    has_right = at < count - 1

    barrier = pltpu.get_barrier_semaphore()
    for d in range(1, groups):
        pl.semaphore_signal(
            barrier, inc=1, device_id={"mode": lax.rem(me + d, groups)}, device_id_type=MESH
        )

    @pl.when(has_left)
    def _():
        pl.semaphore_signal(barrier, inc=1, device_id={"space": at - 1}, device_id_type=MESH)

    @pl.when(has_right)
    def _():
        pl.semaphore_signal(barrier, inc=1, device_id={"space": at + 1}, device_id_type=MESH)

    fields_here = [
        pltpu.make_async_copy(start, start_here, home_sem.at[0]),
        pltpu.make_async_copy(source, source_here, home_sem.at[1]),
    ]
    fetches = [
        pltpu.make_async_copy(triples, triples_here, fetch_sem.at[0]),
        pltpu.make_async_copy(coef, coef_here, fetch_sem.at[1]),
        pltpu.make_async_copy(mean, coefs.at[pl.ds(1, planes), 0], fetch_sem.at[2]),
    ] + [
        pltpu.make_async_copy(
            kl.at[:, z], coefs.at[z + 1, pl.ds(1, nfields - 1)], fetch_sem.at[3 + z]
        )
        for z in range(planes)
    ]
    for copy in fetches:
        copy.start()

    @pl.when(jnp.logical_not(has_left))
    def _():
        coefs[0] = jnp.zeros(coefs.shape[1:], jnp.float32)
        for k in range(2):
            vt[k, 0] = jnp.zeros(vt.shape[2:], jnp.float32)

    @pl.when(jnp.logical_not(has_right))
    def _():
        coefs[planes + 1] = jnp.zeros(coefs.shape[1:], jnp.float32)
        for k in range(2):
            vt[k, planes + 1] = jnp.zeros(vt.shape[2:], jnp.float32)

    @pl.when(me == 0)
    def _():
        for k in range(2):
            for z in range(planes):
                vt[k, z + 1, 0] = jnp.zeros(vt.shape[3:], jnp.float32)

    @pl.when(me == groups - 1)
    def _():
        for k in range(2):
            for z in range(planes):
                vt[k, z + 1, rows + 1] = jnp.zeros(vt.shape[3:], jnp.float32)

    far = lax.rem(at, 2)
    near = 1 - far

    def plane_of(side, i):
        return side * (planes - 1) + (1 - 2 * side) * i

    def band(ref, which):
        return ref.at[:, :, pl.ds(pl.multiple_of(which * rows, rows), rows), :]

    def modes(ref, which):
        size = local * stride
        return ref.at[pl.ds(pl.multiple_of(which * size, size), size), :].reshape(
            local, planes, rows, lanes
        )

    def ends(phase, i, target, owner):
        if phase < 2:
            z = plane_of(far, i)
            return (
                band((start, source)[phase], target).at[:, z],
                modes((in_first, in_second)[phase], owner).at[:, z],
            )
        z = plane_of(near, i)
        return (
            modes((out_first, out_second)[phase - 2], target).at[:, z],
            band((a_first, a_second)[phase - 2], owner).at[:, z],
        )

    def remote(phase, i, d):
        peer = lax.rem(me + d, groups)
        src, dst = ends(phase, i, peer, me)
        part = phase * planes + i
        return pltpu.make_async_remote_copy(
            src_ref=src, dst_ref=dst,
            send_sem=trade_send.at[part, d - 1], recv_sem=trade_recv.at[part, d - 1],
            device_id={"mode": peer}, device_id_type=MESH,
        )

    def own(phase, i):
        src, dst = ends(phase, i, me, me)
        return pltpu.make_async_copy(src, dst, own_sem.at[phase * planes + i])

    def trade_start(phase, i, after=None):
        for d in range(1, groups):
            if after is not None:
                remote(*after, d).wait_send()
            remote(phase, i, d).start()
        own(phase, i).start()

    def trade_wait_send(phase, i):
        for d in range(1, groups):
            remote(phase, i, d).wait_send()

    def trade_wait_recv(phase, i):
        for d in range(1, groups):
            remote(phase, i, d).wait_recv()
        own(phase, i).wait()

    def plane_copy(k, side):
        src, dst = 1 + side * (planes - 1), (planes + 1) * (1 - side)
        inner = (lambda z: coefs.at[z]) if k == 2 else (lambda z: vt.at[k, z, pl.ds(1, rows)])
        return pltpu.make_async_remote_copy(
            src_ref=inner(src), dst_ref=inner(dst),
            send_sem=plane_send.at[k, side], recv_sem=plane_recv.at[k, side],
            device_id={"space": at - 1 + 2 * side}, device_id_type=MESH,
        )

    def has(side):
        other = at - 1 + 2 * side
        return jnp.logical_and(other >= 0, other < count)

    def plane_start(k, side):
        @pl.when(has(side))
        def _():
            plane_copy(k, side).start()

    def plane_wait_send(k):
        for side in range(2):
            @pl.when(has(side))
            def _():
                plane_copy(k, side).wait_send()

    def plane_wait_recv(k, side):
        @pl.when(has(side))
        def _():
            plane_copy(k, 1 - side).wait_recv()

    has_up = me > 0
    has_down = me < groups - 1

    def row_copy(k, z, side):
        src, dst = (1, rows + 1) if side == 0 else (rows, 0)
        return pltpu.make_async_remote_copy(
            src_ref=vt.at[k, z + 1, src], dst_ref=vt.at[k, z + 1, dst],
            send_sem=row_send.at[k, z, side], recv_sem=row_recv.at[k, z, side],
            device_id={"mode": me - 1 if side == 0 else me + 1}, device_id_type=MESH,
        )

    def row_start(k, z):
        for side, sends in ((0, has_up), (1, has_down)):
            @pl.when(sends)
            def _():
                row_copy(k, z, side).start()

    def row_wait_send(k, z):
        for side, sends in ((0, has_up), (1, has_down)):
            @pl.when(sends)
            def _():
                row_copy(k, z, side).wait_send()

    def row_wait_recv(k, z):
        for side, gets in ((0, has_down), (1, has_up)):
            @pl.when(gets)
            def _():
                row_copy(k, z, side).wait_recv()

    pl.semaphore_wait(
        barrier, groups - 1 + has_left.astype(jnp.int32) + has_right.astype(jnp.int32)
    )
    trade_start(0, 0)
    for copy in fetches:
        copy.wait()
    for copy in fields_here:
        copy.start()
    plane_start(2, 0)
    plane_start(2, 1)

    nnz = coef_here.shape[1]
    width = cmat.shape[1]
    fields_row, rows_row, cols_row = (triples_here[i:i + 1, :] for i in range(3))
    coef_row = coef_here[...]
    row_hot = lax.broadcasted_iota(jnp.int32, (padded, nnz), 0) == rows_row
    key_hot = lax.broadcasted_iota(jnp.int32, (width, nnz), 0) == fields_row * padded + cols_row
    coef_high = coef_row.astype(jnp.bfloat16).astype(jnp.float32)
    row_one = jnp.where(row_hot, 1.0, 0.0).astype(jnp.bfloat16)
    for piece, value in enumerate((coef_high, coef_row - coef_high)):
        spread = jnp.where(key_hot, value, 0.0).astype(jnp.bfloat16)
        part = lax.dot_general(
            row_one, spread, (((1,), (1,)), ((), ())), preferred_element_type=jnp.float32
        )
        cmat[piece * padded:(piece + 1) * padded, :] = part.astype(jnp.bfloat16)
    diag = jnp.sum(
        jnp.where(jnp.logical_and(row_hot, fields_row == 0), coef_row, 0.0), axis=1, keepdims=True
    )
    real = lax.broadcasted_iota(jnp.int32, (padded, 1), 0) < slots
    diag = jnp.where(real, diag, 1.0)
    own_ids = lax.broadcasted_iota(jnp.int32, (own_step.shape[0], nnz), 0)
    own_diag = jnp.sum(
        jnp.where(jnp.logical_and(own_ids + me * local == rows_row, fields_row == 0), coef_row, 0.0),
        axis=1, keepdims=True,
    )
    own_diag = jnp.where(own_ids[:, :1] < local, own_diag, 1.0)
    own_step[...] = jnp.broadcast_to(0.8 / own_diag, own_step.shape)
    step = 0.8 / diag

    fill = jnp.zeros((padded - slots, lanes), jnp.float32)

    def fetch(ref, z, y):
        return ref[pl.ds(z * rows + y, slots, stride=stride), :]

    def spread_weights(z, y):
        base = pl.multiple_of((z * height + me * rows + y) * entries, 8)
        return weights[pl.ds(base, entries), :]

    def fill_plane(k, i, one_row):
        z = plane_of(far, i)
        one_row(z, 0)
        one_row(z, rows - 1)
        row_start(k, z)

        def inner(y, carry):
            one_row(z, y)
            return carry
        lax.fori_loop(1, rows - 1, inner, 0)
        if i == 0:
            plane_start(k, far)
        if i == planes - 1:
            plane_start(k, near)

    def relay(z, y):
        vt[0, z + 1, y + 1] = jnp.concatenate([fetch(in_first, z, y), fill], axis=0)

    for i in range(1, planes):
        trade_start(0, i)

    plane_wait_recv(2, 0)
    plane_wait_recv(2, 1)
    lane = lax.broadcasted_iota(jnp.int32, (height, lanes), 1)
    row = lax.broadcasted_iota(jnp.int32, (height, lanes), 0)
    for z in range(planes):
        for m in range(nfields):
            c = coefs[z + 1, m]
            faces = []
            for axis, size, ids in ((1, lanes, lane), (0, height, row)):
                for shift, edge in ((size - 1, size - 1), (1, 0)):
                    other = jnp.where(ids == edge, 0.0, pltpu.roll(c, shift, axis))
                    faces.append(0.5 * (c + other))
            faces.append(0.5 * (c + coefs[z + 2, m]))
            faces.append(0.5 * (c + coefs[z, m]))
            total = functools.reduce(lambda a, b: a + b, faces)
            faces[0] = jnp.where(lane == lanes - 1, 0.0, faces[0])
            faces[1] = jnp.where(lane == 0, 0.0, faces[1])
            first = z * height * entries
            for f, value in enumerate(faces + [total]):
                weights[pl.ds(first + f * nfields + m, height, stride=entries), :] = value
            if m == 0:
                inverse_total[z] = 1.0 / total
                weights[pl.ds(first + (FACES + 1) * nfields, height, stride=entries), :] = (
                    inverse_total[z]
                )

    last = planes - 1
    for i in range(planes):
        trade_wait_recv(0, i)
        fill_plane(0, i, relay)
        trade_start(1, i, after=(0, i))

    def applied(k, z, y):
        w = spread_weights(z, y)
        centre = vt[k, z + 1, y + 1]
        others = (
            pltpu.roll(centre, lanes - 1, 1), pltpu.roll(centre, 1, 1),
            vt[k, z + 1, y + 2], vt[k, z + 1, y],
            vt[k, z + 2, y + 1], vt[k, z, y + 1],
        )
        parts = []
        for m in range(nfields):
            at_total = FACES * nfields + m
            value = w[at_total:at_total + 1] * centre
            for f in range(FACES):
                at_face = f * nfields + m
                value = value - w[at_face:at_face + 1] * others[f]
            parts.append(value)
        if width > nfields * padded:
            parts.append(jnp.zeros((width - nfields * padded, lanes), jnp.float32))
        return jnp.concatenate(parts, axis=0)

    def product(k, z, y):
        x = jnp.concatenate([applied(k, z, y), applied(k, z, y + 1)], axis=1)
        high = x.astype(jnp.bfloat16)
        low = (x - high.astype(jnp.float32)).astype(jnp.bfloat16)
        both = jnp.dot(cmat[...], high, preferred_element_type=jnp.float32)
        rest = jnp.dot(cmat[:padded, :], low, preferred_element_type=jnp.float32)
        return both[:padded] + (both[padded:] + rest)

    def sweep(k, i, out, first_group, groups_here, step_here):
        z = plane_of(near, i)

        def group(t, carry):
            y = 4 * (first_group + step_here * t)
            values = [product(k, z, y), product(k, z, y + 2)]
            for j in range(4):
                out[pl.ds(z * rows + y + j, slots, stride=stride), :] = values[j // 2][
                    :slots, (j % 2) * lanes:(j % 2 + 1) * lanes
                ]
            return carry
        lax.fori_loop(0, groups_here, group, 0)

    def sweep_all(k, out, done):
        quads = rows // 4
        for i in range(planes):
            if i == 0:
                plane_wait_recv(k, near)
            if i == last:
                plane_wait_recv(k, far)
            sweep(k, i, out, 1, quads - 2, 1)
        for i in range(planes):
            row_wait_recv(k, plane_of(near, i))
            sweep(k, i, out, 0, 2, quads - 1)
            done(i)

    sweep_all(0, out_first, lambda i: trade_start(2, i) if i == 0 else None)

    def update(z, y):
        inverse = spread_weights(z, y)[(FACES + 1) * nfields:(FACES + 1) * nfields + 1]
        first = fetch(in_second, z, y) - fetch(out_first, z, y)
        first = jnp.concatenate([first, fill], axis=0)
        vt[1, z + 1, y + 1] = vt[0, z + 1, y + 1] + first * (step * inverse)

    for i in range(planes):
        trade_wait_recv(1, i)
        fill_plane(1, i, update)
        if i == 0:
            trade_wait_send(1, 0)
        else:
            trade_start(2, i, after=(1, i))
    sweep_all(1, out_second, lambda i: trade_start(3, i))

    for copy in fields_here:
        copy.wait()
    for i in range(planes):
        trade_wait_recv(2, i)

    def make_middle(j, carry):
        gain = own_step[pl.ds(j, 1), :]
        for z in range(planes):
            first = source_here[j, z] - a_first[j, z]
            start_here[j, z] = start_here[j, z] + first * (gain * inverse_total[z])
        return carry
    lax.fori_loop(0, local, make_middle, 0)

    def results(i):
        z = plane_of(near, i)
        return [
            pltpu.make_async_copy(held.at[:, z], out.at[:, z], out_sem.at[i, n])
            for n, (held, out) in enumerate(((start_here, smoothed_out), (a_second, residual_out)))
        ]

    for i in range(planes):
        z = plane_of(near, i)
        trade_wait_recv(3, i)

        def make_outputs(j, carry):
            residual = source_here[j, z] - a_second[j, z]
            a_second[j, z] = residual
            gain = own_step[pl.ds(j, 1), :] * inverse_total[z]
            start_here[j, z] = start_here[j, z] + residual * gain
            return carry
        lax.fori_loop(0, local, make_outputs, 0)
        for copy in results(i):
            copy.start()
    for k in range(3):
        plane_wait_send(k)
        if k < 2:
            for z in range(planes):
                row_wait_send(k, z)
    for phase in (2, 3):
        for i in range(planes):
            trade_wait_send(phase, i)
    for i in range(planes):
        for copy in results(i):
            copy.wait()


def place(smoothed, residual, smoothed_out, residual_out, held, sem):
    triples = [
        (ref.at[j], held.at[n, j], out.at[j], sem.at[n, j])
        for j in range(smoothed.shape[0])
        for n, (ref, out) in enumerate(((smoothed, smoothed_out), (residual, residual_out)))
    ]
    inward = [pltpu.make_async_copy(ref, kept, which.at[0]) for ref, kept, _, which in triples]
    outward = [pltpu.make_async_copy(kept, out, which.at[1]) for _, kept, out, which in triples]
    for copy in inward:
        copy.start()
    for arriving, leaving in zip(inward, outward):
        arriving.wait()
        leaving.start()
    for copy in outward:
        copy.wait()


def body(count, start_field, source, mean_field, kl_fields, triples, coef):
    local, planes, height, lanes = start_field.shape
    groups = lax.axis_size("mode")
    slots = local * groups
    nfields = kl_fields.shape[0] + 1
    rows = height // groups
    padded = round_up(slots, 8)
    width = round_up(nfields * padded, 16)
    entries = round_up((FACES + 1) * nfields + 1, 8)
    nnz = triples.shape[0]
    f32 = jnp.float32
    whole = jax.ShapeDtypeStruct(start_field.shape, f32)
    anywhere = pl.BlockSpec(memory_space=pl.ANY)
    dma = pltpu.SemaphoreType.DMA
    smoothed, residual = pl.pallas_call(
        functools.partial(kernel, groups, count),
        out_shape=(whole, whole),
        in_specs=[pl.BlockSpec(memory_space=pltpu.HBM)] * 6,
        out_specs=(anywhere, anywhere),
        scratch_shapes=[
            *[pltpu.VMEM(start_field.shape, f32)] * 4,
            pltpu.VMEM((planes, height, lanes), f32),
            pltpu.VMEM((round_up(local, 8), lanes), f32),
            pltpu.VMEM((3, nnz), jnp.int32),
            pltpu.VMEM((1, nnz), f32),
            pltpu.VMEM((planes + 2, nfields, height, lanes), f32),
            pltpu.VMEM((planes * height * entries, lanes), f32),
            pltpu.VMEM((slots * planes * rows, lanes), f32),
            pltpu.VMEM((slots * planes * rows, lanes), f32),
            pltpu.VMEM((slots * planes * rows, lanes), f32),
            pltpu.VMEM((slots * planes * rows, lanes), f32),
            pltpu.VMEM((2, planes + 2, rows + 2, padded, lanes), f32),
            pltpu.VMEM((2 * padded, width), jnp.bfloat16),
            dma((4 * planes, groups - 1)), dma((4 * planes, groups - 1)), dma((4 * planes,)),
            dma((3 + planes,)), dma((2,)), dma((planes, 2)),
            dma((3, 2)), dma((3, 2)), dma((2, planes, 2)), dma((2, planes, 2)),
        ],
        compiler_params=pltpu.CompilerParams(
            collective_id=0, has_side_effects=True, vmem_limit_bytes=62 * 1024 * 1024
        ),
        name="sweeps",
    )(triples.T, coef[None], start_field, source, mean_field, kl_fields)
    return pl.pallas_call(
        place,
        out_shape=(whole, whole),
        in_specs=[anywhere, anywhere],
        out_specs=(anywhere, anywhere),
        scratch_shapes=[pltpu.VMEM((2, *start_field.shape), f32), dma((2, local, 2))],
        compiler_params=pltpu.CompilerParams(vmem_limit_bytes=62 * 1024 * 1024),
        name="place",
    )(smoothed, residual)


def solution(mesh):
    return jax.shard_map(
        functools.partial(body, mesh.shape["space"]),
        mesh=mesh,
        in_specs=(
            P("mode", "space", None, None),
            P("mode", "space", None, None),
            P("space", None, None),
            P(None, "space", None, None),
            P(),
            P(),
        ),
        out_specs=(P("mode", "space", None, None), P("mode", "space", None, None)),
        check_vma=False,
    )
```

```python
import functools

import jax
import jax.numpy as jnp
from jax import lax
from jax.experimental import pallas as pl
from jax.experimental.pallas import tpu as pltpu
from jax.sharding import PartitionSpec as P

MESH = pl.DeviceIdType.MESH
FACES = 6


def round_up(value, multiple):
    return -(-value // multiple) * multiple


def kernel(
    groups, count, triples, coef, start, source, mean, kl,
    smoothed_out, residual_out,
    start_here, source_here, a_first, a_second, inverse_total, own_step,
    triples_here, coef_here, coefs, weights, in_first, in_second, out_first, out_second, vt, cmat,
    trade_send, trade_recv, own_sem, fetch_sem, home_sem, out_sem, plane_send, plane_recv, row_send, row_recv,
):
    local, planes, height, lanes = start.shape
    slots = local * groups
    rows = height // groups
    nfields = kl.shape[0] + 1
    padded = vt.shape[3]
    entries = weights.shape[0] // (planes * height)
    stride = planes * rows
    me = lax.axis_index("mode")
    at = lax.axis_index("space")
    has_left = at > 0
    has_right = at < count - 1

    barrier = pltpu.get_barrier_semaphore()
    for d in range(1, groups):
        pl.semaphore_signal(
            barrier, inc=1, device_id={"mode": lax.rem(me + d, groups)}, device_id_type=MESH
        )

    @pl.when(has_left)
    def _():
        pl.semaphore_signal(barrier, inc=1, device_id={"space": at - 1}, device_id_type=MESH)

    @pl.when(has_right)
    def _():
        pl.semaphore_signal(barrier, inc=1, device_id={"space": at + 1}, device_id_type=MESH)

    fields_here = [
        pltpu.make_async_copy(start, start_here, home_sem.at[0]),
        pltpu.make_async_copy(source, source_here, home_sem.at[1]),
    ]
    fetches = [
        pltpu.make_async_copy(triples, triples_here, fetch_sem.at[0]),
        pltpu.make_async_copy(coef, coef_here, fetch_sem.at[1]),
        pltpu.make_async_copy(mean, coefs.at[pl.ds(1, planes), 0], fetch_sem.at[2]),
    ] + [
        pltpu.make_async_copy(
            kl.at[:, z], coefs.at[z + 1, pl.ds(1, nfields - 1)], fetch_sem.at[3 + z]
        )
        for z in range(planes)
    ]
    for copy in fetches:
        copy.start()

    @pl.when(jnp.logical_not(has_left))
    def _():
        coefs[0] = jnp.zeros(coefs.shape[1:], jnp.float32)
        for k in range(2):
            vt[k, 0] = jnp.zeros(vt.shape[2:], jnp.float32)

    @pl.when(jnp.logical_not(has_right))
    def _():
        coefs[planes + 1] = jnp.zeros(coefs.shape[1:], jnp.float32)
        for k in range(2):
            vt[k, planes + 1] = jnp.zeros(vt.shape[2:], jnp.float32)

    @pl.when(me == 0)
    def _():
        for k in range(2):
            for z in range(planes):
                vt[k, z + 1, 0] = jnp.zeros(vt.shape[3:], jnp.float32)

    @pl.when(me == groups - 1)
    def _():
        for k in range(2):
            for z in range(planes):
                vt[k, z + 1, rows + 1] = jnp.zeros(vt.shape[3:], jnp.float32)

    far = lax.rem(at, 2)
    near = 1 - far

    def plane_of(side, i):
        return side * (planes - 1) + (1 - 2 * side) * i

    def band(ref, which):
        return ref.at[:, :, pl.ds(pl.multiple_of(which * rows, rows), rows), :]

    def modes(ref, which):
        size = local * stride
        return ref.at[pl.ds(pl.multiple_of(which * size, size), size), :].reshape(
            local, planes, rows, lanes
        )

    def ends(phase, i, target, owner):
        if phase < 2:
            z = plane_of(far, i)
            return (
                band((start, source)[phase], target).at[:, z],
                modes((in_first, in_second)[phase], owner).at[:, z],
            )
        z = plane_of(near, i)
        return (
            modes((out_first, out_second)[phase - 2], target).at[:, z],
            band((a_first, a_second)[phase - 2], owner).at[:, z],
        )

    def remote(phase, i, d):
        peer = lax.rem(me + d, groups)
        src, dst = ends(phase, i, peer, me)
        part = phase * planes + i
        return pltpu.make_async_remote_copy(
            src_ref=src, dst_ref=dst,
            send_sem=trade_send.at[part, d - 1], recv_sem=trade_recv.at[part, d - 1],
            device_id={"mode": peer}, device_id_type=MESH,
        )

    def own(phase, i):
        src, dst = ends(phase, i, me, me)
        return pltpu.make_async_copy(src, dst, own_sem.at[phase * planes + i])

    def trade_start(phase, i, after=None):
        for d in range(1, groups):
            if after is not None:
                remote(*after, d).wait_send()
            remote(phase, i, d).start()
        own(phase, i).start()

    def trade_wait_send(phase, i):
        for d in range(1, groups):
            remote(phase, i, d).wait_send()

    def trade_wait_recv(phase, i):
        for d in range(1, groups):
            remote(phase, i, d).wait_recv()
        own(phase, i).wait()

    def plane_copy(k, side):
        src, dst = 1 + side * (planes - 1), (planes + 1) * (1 - side)
        inner = (lambda z: coefs.at[z]) if k == 2 else (lambda z: vt.at[k, z, pl.ds(1, rows)])
        return pltpu.make_async_remote_copy(
            src_ref=inner(src), dst_ref=inner(dst),
            send_sem=plane_send.at[k, side], recv_sem=plane_recv.at[k, side],
            device_id={"space": at - 1 + 2 * side}, device_id_type=MESH,
        )

    def has(side):
        other = at - 1 + 2 * side
        return jnp.logical_and(other >= 0, other < count)

    def plane_start(k, side):
        @pl.when(has(side))
        def _():
            plane_copy(k, side).start()

    def plane_wait_send(k):
        for side in range(2):
            @pl.when(has(side))
            def _():
                plane_copy(k, side).wait_send()

    def plane_wait_recv(k, side):
        @pl.when(has(side))
        def _():
            plane_copy(k, 1 - side).wait_recv()

    has_up = me > 0
    has_down = me < groups - 1

    def row_copy(k, z, side):
        src, dst = (1, rows + 1) if side == 0 else (rows, 0)
        return pltpu.make_async_remote_copy(
            src_ref=vt.at[k, z + 1, src], dst_ref=vt.at[k, z + 1, dst],
            send_sem=row_send.at[k, z, side], recv_sem=row_recv.at[k, z, side],
            device_id={"mode": me - 1 if side == 0 else me + 1}, device_id_type=MESH,
        )

    def row_start(k, z):
        for side, sends in ((0, has_up), (1, has_down)):
            @pl.when(sends)
            def _():
                row_copy(k, z, side).start()

    def row_wait_send(k, z):
        for side, sends in ((0, has_up), (1, has_down)):
            @pl.when(sends)
            def _():
                row_copy(k, z, side).wait_send()

    def row_wait_recv(k, z):
        for side, gets in ((0, has_down), (1, has_up)):
            @pl.when(gets)
            def _():
                row_copy(k, z, side).wait_recv()

    pl.semaphore_wait(
        barrier, groups - 1 + has_left.astype(jnp.int32) + has_right.astype(jnp.int32)
    )
    trade_start(0, 0)
    for copy in fetches:
        copy.wait()
    for copy in fields_here:
        copy.start()
    plane_start(2, 0)
    plane_start(2, 1)

    nnz = coef_here.shape[1]
    width = cmat.shape[1]
    fields_row, rows_row, cols_row = (triples_here[i:i + 1, :] for i in range(3))
    coef_row = coef_here[...]
    row_hot = lax.broadcasted_iota(jnp.int32, (padded, nnz), 0) == rows_row
    key_hot = lax.broadcasted_iota(jnp.int32, (width, nnz), 0) == fields_row * padded + cols_row
    coef_high = coef_row.astype(jnp.bfloat16).astype(jnp.float32)
    row_one = jnp.where(row_hot, 1.0, 0.0).astype(jnp.bfloat16)
    for piece, value in enumerate((coef_high, coef_row - coef_high)):
        spread = jnp.where(key_hot, value, 0.0).astype(jnp.bfloat16)
        part = lax.dot_general(
            row_one, spread, (((1,), (1,)), ((), ())), preferred_element_type=jnp.float32
        )
        cmat[piece * padded:(piece + 1) * padded, :] = part.astype(jnp.bfloat16)
    diag = jnp.sum(
        jnp.where(jnp.logical_and(row_hot, fields_row == 0), coef_row, 0.0), axis=1, keepdims=True
    )
    real = lax.broadcasted_iota(jnp.int32, (padded, 1), 0) < slots
    diag = jnp.where(real, diag, 1.0)
    own_ids = lax.broadcasted_iota(jnp.int32, (own_step.shape[0], nnz), 0)
    own_diag = jnp.sum(
        jnp.where(jnp.logical_and(own_ids + me * local == rows_row, fields_row == 0), coef_row, 0.0),
        axis=1, keepdims=True,
    )
    own_diag = jnp.where(own_ids[:, :1] < local, own_diag, 1.0)
    own_step[...] = jnp.broadcast_to(0.8 / own_diag, own_step.shape)
    step = 0.8 / diag

    fill = jnp.zeros((padded - slots, lanes), jnp.float32)

    def fetch(ref, z, y):
        return ref[pl.ds(z * rows + y, slots, stride=stride), :]

    def spread_weights(z, y):
        base = pl.multiple_of((z * height + me * rows + y) * entries, 8)
        return weights[pl.ds(base, entries), :]

    def fill_plane(k, i, one_row):
        z = plane_of(far, i)
        one_row(z, 0)
        one_row(z, rows - 1)
        row_start(k, z)

        def inner(y, carry):
            one_row(z, y)
            return carry
        lax.fori_loop(1, rows - 1, inner, 0, unroll=7)
        if i == 0:
            plane_start(k, far)
        if i == planes - 1:
            plane_start(k, near)

    def relay(z, y):
        vt[0, z + 1, y + 1] = jnp.concatenate([fetch(in_first, z, y), fill], axis=0)

    for i in range(1, planes):
        trade_start(0, i)

    plane_wait_recv(2, 0)
    plane_wait_recv(2, 1)
    lane = lax.broadcasted_iota(jnp.int32, (height, lanes), 1)
    row = lax.broadcasted_iota(jnp.int32, (height, lanes), 0)
    for z in range(planes):
        for m in range(nfields):
            c = coefs[z + 1, m]
            faces = []
            for axis, size, ids in ((1, lanes, lane), (0, height, row)):
                for shift, edge in ((size - 1, size - 1), (1, 0)):
                    other = jnp.where(ids == edge, 0.0, pltpu.roll(c, shift, axis))
                    faces.append(0.5 * (c + other))
            faces.append(0.5 * (c + coefs[z + 2, m]))
            faces.append(0.5 * (c + coefs[z, m]))
            total = functools.reduce(lambda a, b: a + b, faces)
            faces[0] = jnp.where(lane == lanes - 1, 0.0, faces[0])
            faces[1] = jnp.where(lane == 0, 0.0, faces[1])
            first = z * height * entries
            for f, value in enumerate(faces + [total]):
                weights[pl.ds(first + f * nfields + m, height, stride=entries), :] = value
            if m == 0:
                inverse_total[z] = 1.0 / total
                weights[pl.ds(first + (FACES + 1) * nfields, height, stride=entries), :] = (
                    inverse_total[z]
                )

    last = planes - 1
    for i in range(planes):
        trade_wait_recv(0, i)
        fill_plane(0, i, relay)
        trade_start(1, i, after=(0, i))

    def applied(k, z, y):
        w = spread_weights(z, y)
        centre = vt[k, z + 1, y + 1]
        others = (
            pltpu.roll(centre, lanes - 1, 1), pltpu.roll(centre, 1, 1),
            vt[k, z + 1, y + 2], vt[k, z + 1, y],
            vt[k, z + 2, y + 1], vt[k, z, y + 1],
        )
        parts = []
        for m in range(nfields):
            at_total = FACES * nfields + m
            value = w[at_total:at_total + 1] * centre
            for f in range(FACES):
                at_face = f * nfields + m
                value = value - w[at_face:at_face + 1] * others[f]
            parts.append(value)
        if width > nfields * padded:
            parts.append(jnp.zeros((width - nfields * padded, lanes), jnp.float32))
        return jnp.concatenate(parts, axis=0)

    def product(k, z, y):
        x = jnp.concatenate([applied(k, z, y), applied(k, z, y + 1)], axis=1)
        high = x.astype(jnp.bfloat16)
        low = (x - high.astype(jnp.float32)).astype(jnp.bfloat16)
        both = jnp.dot(cmat[...], high, preferred_element_type=jnp.float32)
        rest = jnp.dot(cmat[:padded, :], low, preferred_element_type=jnp.float32)
        return both[:padded] + (both[padded:] + rest)

    def sweep(k, i, out, first_group, groups_here, step_here):
        z = plane_of(near, i)

        def group(t, carry):
            y = 4 * (first_group + step_here * t)
            values = [product(k, z, y), product(k, z, y + 2)]
            for j in range(4):
                out[pl.ds(z * rows + y + j, slots, stride=stride), :] = values[j // 2][
                    :slots, (j % 2) * lanes:(j % 2 + 1) * lanes
                ]
            return carry
        lax.fori_loop(0, groups_here, group, 0)

    def sweep_all(k, out, done):
        quads = rows // 4
        for i in range(planes):
            if i == 0:
                plane_wait_recv(k, near)
            if i == last:
                plane_wait_recv(k, far)
            sweep(k, i, out, 1, quads - 2, 1)
        for i in range(planes):
            row_wait_recv(k, plane_of(near, i))
            sweep(k, i, out, 0, 2, quads - 1)
            done(i)

    sweep_all(0, out_first, lambda i: trade_start(2, i) if i == 0 else None)

    def update(z, y):
        inverse = spread_weights(z, y)[(FACES + 1) * nfields:(FACES + 1) * nfields + 1]
        first = fetch(in_second, z, y) - fetch(out_first, z, y)
        first = jnp.concatenate([first, fill], axis=0)
        vt[1, z + 1, y + 1] = vt[0, z + 1, y + 1] + first * (step * inverse)

    for i in range(planes):
        trade_wait_recv(1, i)
        fill_plane(1, i, update)
        if i == 0:
            trade_wait_send(1, 0)
        else:
            trade_start(2, i, after=(1, i))
    sweep_all(1, out_second, lambda i: trade_start(3, i))

    for copy in fields_here:
        copy.wait()
    for i in range(planes):
        trade_wait_recv(2, i)

    def make_middle(j, carry):
        gain = own_step[pl.ds(j, 1), :]
        for z in range(planes):
            first = source_here[j, z] - a_first[j, z]
            start_here[j, z] = start_here[j, z] + first * (gain * inverse_total[z])
        return carry
    lax.fori_loop(0, local, make_middle, 0)

    def results(i):
        z = plane_of(near, i)
        return [
            pltpu.make_async_copy(held.at[:, z], out.at[:, z], out_sem.at[i, n])
            for n, (held, out) in enumerate(((start_here, smoothed_out), (a_second, residual_out)))
        ]

    for i in range(planes):
        z = plane_of(near, i)
        trade_wait_recv(3, i)

        def make_outputs(j, carry):
            residual = source_here[j, z] - a_second[j, z]
            a_second[j, z] = residual
            gain = own_step[pl.ds(j, 1), :] * inverse_total[z]
            start_here[j, z] = start_here[j, z] + residual * gain
            return carry
        lax.fori_loop(0, local, make_outputs, 0)
        for copy in results(i):
            copy.start()
    for k in range(3):
        plane_wait_send(k)
        if k < 2:
            for z in range(planes):
                row_wait_send(k, z)
    for phase in (2, 3):
        for i in range(planes):
            trade_wait_send(phase, i)
    for i in range(planes):
        for copy in results(i):
            copy.wait()


def place(smoothed, residual, smoothed_out, residual_out, held, sem):
    triples = [
        (ref.at[j], held.at[n, j], out.at[j], sem.at[n, j])
        for j in range(smoothed.shape[0])
        for n, (ref, out) in enumerate(((smoothed, smoothed_out), (residual, residual_out)))
    ]
    inward = [pltpu.make_async_copy(ref, kept, which.at[0]) for ref, kept, _, which in triples]
    outward = [pltpu.make_async_copy(kept, out, which.at[1]) for _, kept, out, which in triples]
    for copy in inward:
        copy.start()
    for arriving, leaving in zip(inward, outward):
        arriving.wait()
        leaving.start()
    for copy in outward:
        copy.wait()


def body(count, start_field, source, mean_field, kl_fields, triples, coef):
    local, planes, height, lanes = start_field.shape
    groups = lax.axis_size("mode")
    slots = local * groups
    nfields = kl_fields.shape[0] + 1
    rows = height // groups
    padded = round_up(slots, 8)
    width = round_up(nfields * padded, 16)
    entries = round_up((FACES + 1) * nfields + 1, 8)
    nnz = triples.shape[0]
    f32 = jnp.float32
    whole = jax.ShapeDtypeStruct(start_field.shape, f32)
    anywhere = pl.BlockSpec(memory_space=pl.ANY)
    dma = pltpu.SemaphoreType.DMA
    smoothed, residual = pl.pallas_call(
        functools.partial(kernel, groups, count),
        out_shape=(whole, whole),
        in_specs=[pl.BlockSpec(memory_space=pltpu.HBM)] * 6,
        out_specs=(anywhere, anywhere),
        scratch_shapes=[
            *[pltpu.VMEM(start_field.shape, f32)] * 4,
            pltpu.VMEM((planes, height, lanes), f32),
            pltpu.VMEM((round_up(local, 8), lanes), f32),
            pltpu.VMEM((3, nnz), jnp.int32),
            pltpu.VMEM((1, nnz), f32),
            pltpu.VMEM((planes + 2, nfields, height, lanes), f32),
            pltpu.VMEM((planes * height * entries, lanes), f32),
            pltpu.VMEM((slots * planes * rows, lanes), f32),
            pltpu.VMEM((slots * planes * rows, lanes), f32),
            pltpu.VMEM((slots * planes * rows, lanes), f32),
            pltpu.VMEM((slots * planes * rows, lanes), f32),
            pltpu.VMEM((2, planes + 2, rows + 2, padded, lanes), f32),
            pltpu.VMEM((2 * padded, width), jnp.bfloat16),
            dma((4 * planes, groups - 1)), dma((4 * planes, groups - 1)), dma((4 * planes,)),
            dma((3 + planes,)), dma((2,)), dma((planes, 2)),
            dma((3, 2)), dma((3, 2)), dma((2, planes, 2)), dma((2, planes, 2)),
        ],
        compiler_params=pltpu.CompilerParams(
            collective_id=0, has_side_effects=True, vmem_limit_bytes=62 * 1024 * 1024
        ),
        name="sweeps",
    )(triples.T, coef[None], start_field, source, mean_field, kl_fields)
    return pl.pallas_call(
        place,
        out_shape=(whole, whole),
        in_specs=[anywhere, anywhere],
        out_specs=(anywhere, anywhere),
        scratch_shapes=[pltpu.VMEM((2, *start_field.shape), f32), dma((2, local, 2))],
        compiler_params=pltpu.CompilerParams(vmem_limit_bytes=62 * 1024 * 1024),
        name="place",
    )(smoothed, residual)


def solution(mesh):
    return jax.shard_map(
        functools.partial(body, mesh.shape["space"]),
        mesh=mesh,
        in_specs=(
            P("mode", "space", None, None),
            P("mode", "space", None, None),
            P("space", None, None),
            P(None, "space", None, None),
            P(),
            P(),
        ),
        out_specs=(P("mode", "space", None, None), P("mode", "space", None, None)),
        check_vma=False,
    )
```
